32 devices in a mesh: dp: 16 (over z, y, core), ctx: 2 (over x).
Axes of the slice: x: 2, y: 2, z: 4, core: 2. Of those that a mesh axis runs over, the one named last changes fastest.
Arguments:
- query_heads: bfloat16 [16, 256, 4096], P('dp', 'ctx'), may hold values from -160 to 160
- key_heads: bfloat16 [16, 256, 512], P('dp', 'ctx'), may hold values from -6 to 6
- value_heads: bfloat16 [16, 256, 512], P('dp', 'ctx'), may hold values from -6 to 6
- out_grad: bfloat16 [16, 256, 4096], P('dp', 'ctx'), may hold values from -6 to 6
- layer_inputs: bfloat16 [16, 256, 8192], P('dp', 'ctx'), may hold values from -6 to 6
- doc_lengths: int32 [16, 8], P('dp'), may hold values from 1 to 128, 256 in all within a row
Outputs:
- query_grad: bfloat16 [16, 256, 4096], P('dp', 'ctx')
- key_grad: bfloat16 [16, 256, 512], P('dp', 'ctx')
- value_grad: bfloat16 [16, 256, 512], P('dp', 'ctx')
- weight_grad: float32 [8192, 512], P(('dp', 'ctx'))
The draws below stay inside these ranges and needn't reach their ends.
All inputs are finite; a program needn't handle non-finite values.
Results may differ from the reference program's by a relative error of at most 0.0053.
Values may be sent and summed in bfloat16 or wider, within the bound.
A program may use at most 128 MiB of HBM per device.

```python
import math
import jax
import jax.numpy as jnp
import numpy as np
from jax import lax

D = 8192
HD = 128
HEADS = 32
KVH = 4
DOCS = 8
SEQ = 256
MAXDOC = 128
QW = 4096
KW = 512
N_DP = 16


def shared_keys(key):
    base_keys = jax.random.normal(key, (N_DP, SEQ, KVH, HD), jnp.float32)
    return jnp.clip(base_keys, -6.0, 6.0)


def draw_key_heads(key, part):
    base_keys = shared_keys(key)
    return base_keys.reshape(N_DP, SEQ, KVH * HD).astype(jnp.bfloat16)


def draw_query_heads(key, part):
    key = jax.random.fold_in(key, 7)
    group_size = HEADS // KVH
    draw_shape = (N_DP, SEQ, KVH, group_size, HD)
    entries = jnp.clip(jax.random.normal(key, draw_shape, jnp.float32), -6.0, 6.0)
    return entries.reshape(N_DP, SEQ, HEADS * HD).astype(jnp.bfloat16)


def spiked(values, key, source, target, parts, factor):
    def block_of(dim):
        return (jnp.arange(values.shape[dim]) // (values.shape[dim] // parts)).reshape((-1,) + (1,) * (values.ndim - 1 - dim))

    one_side = jax.random.permutation(key, parts)[block_of(target)]
    second = (block_of(target) + parts // 2) % parts
    return jnp.where((block_of(source) == one_side) | (block_of(source) == second), factor * values, values)


def shard_levels(stream_key, dims, pieces, low, largest):
    gain, own = 1.0, jax.random.fold_in(stream_key, 6)
    for position, shards_of in pieces:
        steps = jnp.exp(jax.random.uniform(jax.random.fold_in(own, position), (shards_of,), jnp.float32, low / len(pieces), largest / len(pieces)))
        gain = gain * jnp.repeat(steps, dims[position] // shards_of).reshape([-1 if axis == position else 1 for axis in range(len(dims))])
    return gain


def profile(count, total, most, slope):
    portions = [(1 << 20) // math.isqrt(grade ** slope) + 1 for grade in range(2, count + 1)]
    surplus, given = total - most - (count - 1), [1] * (count - 1)
    while surplus > 0:
        free = [i for i in range(count - 1) if given[i] < most]
        mass, budget = sum([portions[i] for i in free]), surplus
        for i in free:
            more = min(most - given[i], max(1, budget * portions[i] // mass), surplus)
            given[i] = given[i] + more
            surplus = surplus - more
    return np.array([most] + given)


def ragged_sizes(stream_key, number_of, total, reach, skew):
    if number_of == 2:
        one = jax.random.randint(stream_key, (), max(1, total - reach), min(reach, total - 1) + 1)
        return jnp.stack([one, total - one])
    tallies = jnp.asarray(profile(number_of, total, reach, skew), jnp.int32)
    couples = (number_of - 1) // 2
    giver, receiver = tallies[1:1 + 2 * couples:2], tallies[2:2 + 2 * couples:2]
    slack = jnp.minimum(giver - 1, reach - receiver)
    moved = jax.random.randint(jax.random.fold_in(stream_key, 1), (couples,), 0, 1 << 20) % (slack + 1)
    tallies = tallies.at[1:1 + 2 * couples:2].set(giver - moved).at[2:2 + 2 * couples:2].set(receiver + moved)
    return tallies[jax.random.permutation(jax.random.fold_in(stream_key, 2), number_of)]


def centred(key, dims, spread, bound, pieces=(), kind=jnp.bfloat16):
    loudness = shard_levels(key, dims, pieces, -0.22, 0.18) if pieces else 1.0
    result = jax.random.normal(key, dims, jnp.float32) * spread * loudness
    return jnp.minimum(jnp.maximum(result, -bound), bound).astype(kind)


def bell_draw_with(rng, dims, spread, most, cuts, heavy, held_as=jnp.bfloat16):
    drawn = spread * jax.random.normal(rng, dims, jnp.float32)
    if cuts:
        drawn = drawn * shard_levels(rng, dims, cuts, -0.22, 0.18)
    return jnp.clip(spiked(drawn, jax.random.fold_in(rng, 3), *heavy), -most, most).astype(held_as)


def setup_inputs(seed: int = 0) -> dict:
    streams_of = jax.random.split(jax.random.key(seed), 7)
    return {
        "query_heads": draw_query_heads(jax.random.fold_in(streams_of[6], 71), 0),
        "key_heads": draw_key_heads(jax.random.fold_in(streams_of[6], 71), 0),
        "value_heads": centred(streams_of[2], (N_DP, SEQ, KW), 1.0, 6.0, ((0, 16), (1, 2))),
        "out_grad": centred(streams_of[3], (N_DP, SEQ, QW), 1.0, 6.0, ((0, 16), (1, 2))),
        "layer_inputs": bell_draw_with(streams_of[4], (N_DP, SEQ, D), 1.0, 6.0, ((0, 16), (1, 2)), (0, 2, 16, 2.0)),
        "doc_lengths": jax.vmap(lambda own: ragged_sizes(own, DOCS, SEQ, MAXDOC, 2))(jax.random.split(streams_of[5], N_DP)).reshape((N_DP, DOCS)).astype(jnp.int32),
    }


NEG_FILL = -1e30


def document_ids(lengths_row, length):
    endings = jnp.cumsum(lengths_row).astype(jnp.int32)
    positions = jnp.arange(length, dtype=jnp.int32)
    return jnp.sum((positions[:, None] >= endings[None, :]).astype(jnp.int32), axis=1)


def one_sequence(packed):
    query_rows, key_rows, value_rows, grad_rows, lengths_row = packed
    length = query_rows.shape[0]
    group_size = HEADS // KVH
    softmax_scale = HD ** -0.5
    query_split = query_rows.reshape(length, KVH, group_size, HD).astype(jnp.float32)
    key_split = key_rows.reshape(length, KVH, HD).astype(jnp.float32)
    value_split = value_rows.reshape(length, KVH, HD).astype(jnp.float32)
    grad_split = grad_rows.reshape(length, KVH, group_size, HD).astype(jnp.float32)
    documents = document_ids(lengths_row, length)
    positions = jnp.arange(length, dtype=jnp.int32)
    allowed = (documents[:, None] == documents[None, :]) & (positions[None, :] <= positions[:, None])
    scores = jnp.einsum("igsd,jgd->gsij", query_split, key_split) * softmax_scale
    scores = jnp.where(allowed[None, None], scores, NEG_FILL)
    row_top = jnp.max(scores, axis=-1, keepdims=True)
    row_total = jnp.sum(jnp.exp(scores - row_top), axis=-1, keepdims=True)
    row_lse = row_top + jnp.log(row_total)
    probability = jnp.exp(scores - row_lse)
    prob_low = lax.optimization_barrier(probability.astype(jnp.bfloat16)).astype(jnp.float32)
    attended = jnp.einsum("gsij,jgd->igsd", prob_low, value_split)
    delta = jnp.transpose(jnp.sum(grad_split * attended, axis=-1), (1, 2, 0))
    dprob = jnp.einsum("igsd,jgd->gsij", grad_split, value_split)
    dscore = probability * (dprob - delta[..., None])
    dscore_low = lax.optimization_barrier(dscore.astype(jnp.bfloat16)).astype(jnp.float32)
    query_grad = jnp.einsum("gsij,jgd->igsd", dscore_low, key_split) * softmax_scale
    key_grad = jnp.einsum("gsij,igsd->jgd", dscore_low, query_split) * softmax_scale
    value_grad = jnp.einsum("gsij,igsd->jgd", prob_low, grad_split)
    return (query_grad.reshape(length, HEADS * HD).astype(jnp.bfloat16),
            key_grad.reshape(length, KVH * HD).astype(jnp.bfloat16),
            value_grad.reshape(length, KVH * HD).astype(jnp.bfloat16))


def reference(query_heads, key_heads, value_heads, out_grad, layer_inputs, doc_lengths):
    query_grad, key_grad, value_grad = lax.map(one_sequence, (query_heads, key_heads, value_heads, out_grad, doc_lengths))
    width = layer_inputs.shape[2]
    key_width = key_heads.shape[2]

    def add_sequence(running, pair):
        input_rows, grad_rows = pair
        term = jnp.dot(input_rows.T, grad_rows, preferred_element_type=jnp.float32)
        return running + term, None

    start_grad = jnp.zeros((width, key_width), jnp.float32)
    weight_grad, unused_rest = lax.scan(add_sequence, start_grad, (layer_inputs, value_grad))
    token_total = layer_inputs.shape[0] * layer_inputs.shape[1]
    weight_grad = weight_grad * (token_total ** -0.5)
    return (query_grad, key_grad, value_grad, weight_grad)
```

```python
import functools

import jax
import jax.numpy as jnp
from jax import lax
from jax.experimental import pallas as pl
from jax.experimental.pallas import tpu as pltpu
from jax.sharding import PartitionSpec as P

HD = 128
HEADS = 32
KVH = 4
GROUP = HEADS // KVH
PAIR = 2
PLANE = 8
F32 = jnp.float32
BF16 = jnp.bfloat16
MESH = pl.DeviceIdType.MESH


NEG_FILL = -1e30


def nt(a, b):
    return lax.dot_general(a, b, (((1,), (1,)), ((), ())), preferred_element_type=F32)


def nn(a, b):
    return jnp.dot(a, b, preferred_element_type=F32)


def cols(index, width=HD):
    return pl.ds(pl.multiple_of(index * width, width), width)


def target_orders(depth):
    table = []
    for z in range(depth):
        up = list(range(depth - 1, z, -1))
        down = list(range(z))
        first, second = (up, down) if z < depth // 2 else (down, up)
        order = []
        while first or second:
            if first:
                order.append(first.pop(0))
            if second:
                order.append(second.pop(0))
        table.append(order + [z])
    return table


def documents_of(lengths, shape, axis, first):
    positions = lax.broadcasted_iota(jnp.int32, shape, axis) + first
    found = jnp.zeros(shape, jnp.int32)
    ending = jnp.int32(0)
    for number in range(lengths.shape[1]):
        ending = ending + lengths[0, number]
        found = found + (positions >= ending).astype(jnp.int32)
    return positions, found


def kernel(
    depth, out_scale,
    q_ref, k_ref, v_ref, go_ref, x_ref, len_ref,
    dq_ref, dk_ref, dv_ref, w_ref,
    k_prev, v_prev, bias, term_k, term_v, sum_k, sum_v,
    x_all, dvt_all, w_send, w_recv, w_own,
    kv_send, kv_recv, term_send, term_recv,
    x_send, x_recv, x_local, dv_send, dv_recv, ws_send, ws_recv,
):
    rows = q_ref.shape[0]
    dp = lax.axis_index("dp")
    ctx = lax.axis_index("ctx")
    lanes = PLANE // 2
    z = dp // lanes
    me = (dp % lanes) * 2 + ctx
    width = w_ref.shape[0]
    scale = HD ** -0.5

    def peer(offset):
        other = (me + offset) % PLANE
        return other, (z * lanes + other // 2, other % 2)

    above = (dp + lanes, ctx)
    below = (dp - lanes, ctx)
    partner = (dp, 1 - ctx)
    last = depth - 1

    barrier = pltpu.get_barrier_semaphore()
    for offset in range(1, PLANE):
        pl.semaphore_signal(barrier, inc=1, device_id=peer(offset)[1], device_id_type=MESH)

    @pl.when(z > 0)
    def _():
        pl.semaphore_signal(barrier, inc=1, device_id=below, device_id_type=MESH)

    @pl.when(z < last)
    def _():
        pl.semaphore_signal(barrier, inc=1, device_id=above, device_id_type=MESH)

    line = (z > 0).astype(jnp.int32) + (z < last).astype(jnp.int32)
    pl.semaphore_wait(barrier, PLANE - 1 + line)

    def remote(src, dst, send, recv, device):
        return pltpu.make_async_remote_copy(
            src_ref=src, dst_ref=dst, send_sem=send, recv_sem=recv,
            device_id=device, device_id_type=MESH,
        )

    def kv_copies():
        return (
            remote(k_ref, k_prev, kv_send.at[0], kv_recv.at[0], partner),
            remote(v_ref, v_prev, kv_send.at[1], kv_recv.at[1], partner),
        )

    def term_copy(part):
        buffer = (term_v, term_k)[part]
        return remote(buffer, buffer, term_send.at[part], term_recv.at[part], partner)

    @pl.when(ctx == 0)
    def _():
        for copy in kv_copies():
            copy.start()

    table = target_orders(depth)
    targets = []
    for step in range(depth):
        target = jnp.int32(0)
        for place in range(depth):
            target = target + (z == place).astype(jnp.int32) * table[place][step]
        targets.append(target)

    def x_copy(target, offset, sender, receiver, device):
        return remote(
            x_ref.at[:, cols(target * PLANE + receiver, width)],
            x_all.at[target, pl.ds(pl.multiple_of(sender * rows, rows), rows)],
            x_send.at[target, offset - 1], x_recv.at[target, offset - 1], device,
        )

    def own_copy(target):
        return pltpu.make_async_copy(
            x_ref.at[:, cols(target * PLANE + me, width)],
            x_all.at[target, pl.ds(pl.multiple_of(me * rows, rows), rows)],
            x_local.at[target],
        )

    for target in targets:
        for offset in range(1, PLANE):
            other, device = peer(offset)
            x_copy(target, offset, me, other, device).start()
        own_copy(target).start()

    def attend(blocks):
        length = blocks * rows
        shape = (length, rows)
        first = ctx * rows
        query_pos, query_docs = documents_of(len_ref, shape, 1, first)
        key_pos, key_docs = documents_of(len_ref, shape, 0, first - (blocks - 1) * rows)
        allowed = (query_docs == key_docs) & (key_pos <= query_pos)
        bias[:length] = jnp.where(allowed, 0.0, NEG_FILL)

        def group(g, carry):
            here = cols(g)
            key_part, value_part = k_ref[:, here], v_ref[:, here]
            if blocks == 2:
                key_part = jnp.concatenate([k_prev[:, here], key_part], axis=0)
                value_part = jnp.concatenate([v_prev[:, here], value_part], axis=0)
            key_turned = key_part.astype(F32).T.astype(BF16)
            key_sum = jnp.zeros((length, HD), F32)
            value_sum = jnp.zeros((length, HD), F32)
            mask = jnp.concatenate([bias[:length]] * PAIR, axis=1)
            for pair in range(GROUP // PAIR):
                heads = [cols(g * GROUP + pair * PAIR + i) for i in range(PAIR)]
                query = jnp.concatenate([q_ref[:, h] for h in heads], axis=0)
                grad = jnp.concatenate([go_ref[:, h] for h in heads], axis=0)
                scores = nt(key_part, query) * scale + mask
                top = jnp.max(scores, axis=0, keepdims=True)
                weight = jnp.exp(scores - top)
                prob = weight * (1.0 / jnp.sum(weight, axis=0, keepdims=True))
                prob_low = prob.astype(BF16)
                dprob = nt(value_part, grad)
                delta = jnp.sum(prob_low.astype(F32) * dprob, axis=0, keepdims=True)
                dscore = (prob * (dprob - delta)).astype(BF16)
                value_sum = value_sum + nn(prob_low, grad)
                key_sum = key_sum + nn(dscore, query)
                turned = nn(key_turned, dscore) * scale
                for i, h in enumerate(heads):
                    dq_ref[:, h] = turned[:, i * rows:(i + 1) * rows].T.astype(BF16)
            key_sum = key_sum * scale
            if blocks == 2:
                term_k[:, here] = key_sum[:rows].astype(BF16)
                term_v[:, here] = value_sum[:rows].astype(BF16)
                dk_ref[:, here] = key_sum[rows:].astype(BF16)
                dv_ref[:, here] = value_sum[rows:].astype(BF16)
                dvt_all[here, cols(me, rows)] = value_sum[rows:].T.astype(BF16)
            else:
                sum_k[:, here] = key_sum
                sum_v[:, here] = value_sum
            return carry

        lax.fori_loop(0, KVH, group, 0)

    @pl.when(ctx == 0)
    def _():
        attend(1)
        term_copy(0).wait_recv()
        for g in range(KVH):
            here = pl.ds(g * HD, HD)
            total = sum_v[:, here] + term_v[:, here].astype(F32)
            dv_ref[:, here] = total.astype(BF16)
            dvt_all[here, cols(me, rows)] = total.T.astype(BF16)

    @pl.when(ctx == 1)
    def _():
        for copy in kv_copies():
            copy.wait_recv()
        attend(2)
        for part in range(2):
            term_copy(part).start()

    def dv_copy(offset, sender, device):
        return remote(
            dvt_all.at[:, cols(sender, rows)], dvt_all.at[:, cols(sender, rows)],
            dv_send.at[offset - 1], dv_recv.at[offset - 1], device,
        )

    for offset in range(1, PLANE):
        dv_copy(offset, me, peer(offset)[1]).start()

    @pl.when(ctx == 0)
    def _():
        term_copy(1).wait_recv()
        dk_ref[...] = (sum_k[...] + term_k[...].astype(F32)).astype(BF16)

    for offset in range(1, PLANE):
        sender = (me + PLANE - offset) % PLANE
        dv_copy(offset, sender, peer(offset)[1]).wait_recv()

    def w_up(target):
        return remote(w_send.at[target], w_recv.at[0, target], ws_send.at[target], ws_recv.at[0, target], above)

    def w_down(target):
        return remote(w_send.at[target], w_recv.at[1, target], ws_send.at[target], ws_recv.at[1, target], below)

    for target in targets:
        for offset in range(1, PLANE):
            sender = (me + PLANE - offset) % PLANE
            other, device = peer(offset)
            x_copy(target, offset, sender, me, device).wait_recv()
        own_copy(target).wait()
        w_own[...] = nn(dvt_all[...], x_all[target])

        @pl.when((z > 0) & (target >= z))
        def _():
            w_up(target).wait_recv()
            w_own[...] += w_recv[0, target].astype(F32)

        @pl.when((z < last) & (target <= z))
        def _():
            w_down(target).wait_recv()
            w_own[...] += w_recv[1, target].astype(F32)

        @pl.when(target > z)
        def _():
            w_send[target] = w_own[...].astype(BF16)
            w_up(target).start()

        @pl.when(target < z)
        def _():
            w_send[target] = w_own[...].astype(BF16)
            w_down(target).start()

    w_ref[...] = (w_own[...] * out_scale).T

    for target in targets:
        for offset in range(1, PLANE):
            other, device = peer(offset)
            x_copy(target, offset, me, other, device).wait_send()

        @pl.when(target != z)
        def _():
            w_up(target).wait_send()

    for offset in range(1, PLANE):
        dv_copy(offset, me, peer(offset)[1]).wait_send()

    @pl.when(ctx == 0)
    def _():
        for copy in kv_copies():
            copy.wait_send()

    @pl.when(ctx == 1)
    def _():
        for part in range(2):
            term_copy(part).wait_send()


def fused(query_heads, key_heads, value_heads, out_grad, layer_inputs, doc_lengths):
    rows, model = layer_inputs.shape[1:]
    key_width = key_heads.shape[2]
    count = lax.axis_size("dp") * lax.axis_size("ctx")
    depth = count // PLANE
    width = model // count
    out_scale = (lax.axis_size("dp") * lax.axis_size("ctx") * rows) ** (-0.5)
    vmem = pl.BlockSpec(memory_space=pltpu.VMEM)
    dma = pltpu.SemaphoreType.DMA
    query_grad, key_grad, value_grad, weight_grad = pl.pallas_call(
        functools.partial(kernel, depth, out_scale),
        out_shape=(
            jax.ShapeDtypeStruct(query_heads.shape[1:], BF16),
            jax.ShapeDtypeStruct((rows, key_width), BF16),
            jax.ShapeDtypeStruct((rows, key_width), BF16),
            jax.ShapeDtypeStruct((width, key_width), F32),
        ),
        in_specs=[vmem] * 4 + [pl.BlockSpec(memory_space=pl.ANY), pl.BlockSpec(memory_space=pltpu.SMEM)],
        out_specs=(vmem,) * 4,
        scratch_shapes=[
            pltpu.VMEM((rows, key_width), BF16),
            pltpu.VMEM((rows, key_width), BF16),
            pltpu.VMEM((2 * rows, rows), F32),
            pltpu.VMEM((rows, key_width), BF16),
            pltpu.VMEM((rows, key_width), BF16),
            pltpu.VMEM((rows, key_width), F32),
            pltpu.VMEM((rows, key_width), F32),
            pltpu.VMEM((depth, PLANE * rows, width), BF16),
            pltpu.VMEM((key_width, PLANE * rows), BF16),
            pltpu.VMEM((depth, key_width, width), BF16),
            pltpu.VMEM((2, depth, key_width, width), BF16),
            pltpu.VMEM((key_width, width), F32),
            dma((2,)), dma((2,)), dma((2,)), dma((2,)),
            dma((depth, PLANE - 1)), dma((depth, PLANE - 1)), dma((depth,)),
            dma((PLANE - 1,)), dma((PLANE - 1,)),
            dma((depth,)), dma((2, depth)),
        ],
        compiler_params=pltpu.CompilerParams(
            collective_id=0, has_side_effects=True, vmem_limit_bytes=48 * 1024 * 1024
        ),
    )(query_heads[0], key_heads[0], value_heads[0], out_grad[0], layer_inputs[0], doc_lengths)
    return (query_grad[None], key_grad[None], value_grad[None], weight_grad)


def document_ids(lengths_row, length):
    endings = jnp.cumsum(lengths_row)
    positions = jnp.arange(length, dtype=jnp.int32)
    return jnp.sum((positions[:, None] >= endings[None, :]).astype(jnp.int32), axis=1)


def shards(query_heads, key_heads, value_heads, out_grad, layer_inputs, doc_lengths):
    queries_here = query_heads[0]
    rows_here = queries_here.shape[0]
    shard_count = lax.axis_size("ctx")
    data_count = lax.axis_size("dp")
    length = rows_here * shard_count
    group_size = HEADS // KVH
    softmax_scale = HD ** (-0.5)
    key_width = key_heads.shape[2]
    key_all, value_all = (
        lax.all_gather(key_heads[0], "ctx", axis=0, tiled=True),
        lax.all_gather(value_heads[0], "ctx", axis=0, tiled=True),
    )
    documents = document_ids(doc_lengths[0], length)
    first_row = lax.axis_index("ctx") * rows_here
    positions = jnp.arange(length, dtype=jnp.int32)
    query_pos = first_row + jnp.arange(rows_here, dtype=jnp.int32)
    query_docs = lax.dynamic_slice_in_dim(documents, first_row, rows_here)
    allowed = (query_docs[:, None] == documents[None, :]) & (
        positions[None, :] <= query_pos[:, None]
    )
    query_split = queries_here.reshape(rows_here, KVH, group_size, HD)
    key_split = key_all.reshape(length, KVH, HD)
    value_split = value_all.reshape(length, KVH, HD)
    grad_split = out_grad[0].reshape(rows_here, KVH, group_size, HD)
    scores = (
        jnp.einsum("igsd,jgd->gsij", query_split, key_split, preferred_element_type=jnp.float32)
        * softmax_scale
    )
    scores = jnp.where(allowed[None, None], scores, NEG_FILL)
    row_top = jnp.max(scores, axis=-1, keepdims=True)
    row_total = jnp.sum(jnp.exp(scores - row_top), axis=-1, keepdims=True)
    probability = jnp.exp(scores - (row_top + jnp.log(row_total)))
    prob_low = probability.astype(jnp.bfloat16)
    attended = jnp.einsum(
        "gsij,jgd->igsd", prob_low, value_split, preferred_element_type=jnp.float32
    )
    delta = jnp.transpose(jnp.sum(grad_split.astype(jnp.float32) * attended, axis=-1), (1, 2, 0))
    dprob = jnp.einsum(
        "igsd,jgd->gsij", grad_split, value_split, preferred_element_type=jnp.float32
    )
    dscore_low = (probability * (dprob - delta[..., None])).astype(jnp.bfloat16)
    query_grad = (
        jnp.einsum("gsij,jgd->igsd", dscore_low, key_split, preferred_element_type=jnp.float32)
        * softmax_scale
    )
    query_grad = query_grad.reshape(rows_here, HEADS * HD).astype(jnp.bfloat16)
    key_term = (
        jnp.einsum("gsij,igsd->jgd", dscore_low, query_split, preferred_element_type=jnp.float32)
        * softmax_scale
    )
    value_term = jnp.einsum(
        "gsij,igsd->jgd", prob_low, grad_split, preferred_element_type=jnp.float32
    )
    summed_grads = lax.psum_scatter(
        jnp.concatenate(
            [
                key_term.reshape(lax.axis_size("ctx") * rows_here, key_width),
                value_term.reshape(lax.axis_size("ctx") * rows_here, key_width),
            ],
            axis=1,
        ),
        "ctx",
        scatter_dimension=0,
        tiled=True,
    )
    key_grad = summed_grads[:, :key_width].astype(jnp.bfloat16)
    value_grad = summed_grads[:, key_width:].astype(jnp.bfloat16)
    inputs_here = layer_inputs[0]
    weight_grad = lax.psum_scatter(
        jnp.einsum("te,tc->ec", inputs_here, value_grad, preferred_element_type=jnp.float32),
        ("dp", "ctx"),
        scatter_dimension=0,
        tiled=True,
    )
    weight_grad = weight_grad * (data_count * length) ** (-0.5)
    return (query_grad[None], key_grad[None], value_grad[None], weight_grad)


def place(query_heads, key_heads, value_heads, out_grad, layer_inputs, doc_lengths):
    arrays = (query_heads, key_heads, value_heads, out_grad, layer_inputs, doc_lengths)
    rows, model = layer_inputs.shape[1:]
    count = lax.axis_size("dp") * lax.axis_size("ctx")
    whole_tiles = rows % HD == 0 and model % (count * HD) == 0
    if lax.axis_size("ctx") == 2 and count % PLANE == 0 and whole_tiles:
        return fused(*arrays)
    return shards(*arrays)


def solution(mesh):
    placed = (
        P("dp", "ctx", None),
        P("dp", "ctx", None),
        P("dp", "ctx", None),
        P("dp", "ctx", None),
        P("dp", "ctx", None),
        P("dp", None),
    )
    return jax.shard_map(
        place,
        mesh=mesh,
        in_specs=placed,
        out_specs=(
            P("dp", "ctx", None),
            P("dp", "ctx", None),
            P("dp", "ctx", None),
            P(("dp", "ctx"), None),
        ),
        check_vma=False,
    )
```

```python
import functools
import math

import jax
import jax.numpy as jnp
from jax import lax
from jax.experimental import pallas as pl
from jax.experimental.pallas import tpu as pltpu
from jax.sharding import PartitionSpec as P

HD = 128
HEADS = 32
KVH = 4
GROUP = HEADS // KVH
PAIR = 2
PLANE = 8
LOG2E = math.log2(math.e)
F32 = jnp.float32
BF16 = jnp.bfloat16
MESH = pl.DeviceIdType.MESH


NEG_FILL = -1e30


def nt(a, b):
    return lax.dot_general(a, b, (((1,), (1,)), ((), ())), preferred_element_type=F32)


def nn(a, b):
    return jnp.dot(a, b, preferred_element_type=F32)


def cols(index, width=HD):
    return pl.ds(pl.multiple_of(index * width, width), width)


def target_orders(depth):
    table = []
    for z in range(depth):
        others = [t for t in range(depth) if t != z]
        others.sort(key=lambda t: (-abs(t - z), t))
        table.append(others + [z])
    return table


def documents_of(lengths, shape, axis, first):
    positions = lax.broadcasted_iota(jnp.int32, shape, axis) + first
    found = jnp.zeros(shape, jnp.int32)
    ending = jnp.int32(0)
    for number in range(lengths.shape[1]):
        ending = ending + lengths[0, number]
        found = found + (positions >= ending).astype(jnp.int32)
    return positions, found


def kernel(
    depth, out_scale,
    q_hbm, k_hbm, v_hbm, go_hbm, x_ref, len_ref,
    dq_ref, dk_ref, dv_ref, w_ref,
    q_ref, k_ref, v_ref, go_ref, k_prev, v_prev, bias, term_k, term_v,
    x_all, dvt_all, w_send, w_recv, w_own,
    in_sem, kv_send, kv_recv, term_send, term_recv,
    x_send, x_recv, x_local, dv_send, dv_recv, ws_send, ws_recv,
):
    rows = q_ref.shape[0]
    dp = lax.axis_index("dp")
    ctx = lax.axis_index("ctx")
    lanes = PLANE // 2
    z = dp // lanes
    lane = dp % lanes
    me = lane * 2 + ctx
    width = w_ref.shape[0]
    scale = HD ** -0.5

    inputs = [
        pltpu.make_async_copy(src, dst, in_sem.at[i])
        for i, (src, dst) in enumerate(
            [(k_hbm, k_ref), (v_hbm, v_ref), (q_hbm, q_ref), (go_hbm, go_ref)]
        )
    ]
    for copy in inputs:
        copy.start()

    def peer(offset):
        other = (me + offset) % PLANE
        return other, (z * lanes + other // 2, other % 2)

    def level(target):
        return (target * lanes + lane, ctx)

    partner = (dp, 1 - ctx)

    barrier = pltpu.get_barrier_semaphore()
    for offset in range(1, PLANE):
        pl.semaphore_signal(barrier, inc=1, device_id=peer(offset)[1], device_id_type=MESH)
    for step in range(1, depth):
        pl.semaphore_signal(barrier, inc=1, device_id=level((z + step) % depth), device_id_type=MESH)
    pl.semaphore_wait(barrier, PLANE - 1 + depth - 1)

    def remote(src, dst, send, recv, device):
        return pltpu.make_async_remote_copy(
            src_ref=src, dst_ref=dst, send_sem=send, recv_sem=recv,
            device_id=device, device_id_type=MESH,
        )

    def kv_copy(g, part):
        src, dst = ((k_hbm, k_prev), (v_hbm, v_prev))[part]
        here = cols(g)
        return remote(src.at[:, here], dst.at[:, here], kv_send.at[part, g], kv_recv.at[part, g], partner)

    def term_copy(g, part):
        buffer = (term_v, term_k)[part].at[g]
        return remote(buffer, buffer, term_send.at[part, g], term_recv.at[part, g], partner)

    def x_copy(target, offset, sender, receiver, device):
        return remote(
            x_ref.at[:, cols(target * PLANE + receiver, width)],
            x_all.at[target, pl.ds(pl.multiple_of(sender * rows, rows), rows)],
            x_send.at[target, offset - 1], x_recv.at[target, offset - 1], device,
        )

    def own_copy(target):
        return pltpu.make_async_copy(
            x_ref.at[:, cols(target * PLANE + me, width)],
            x_all.at[target, pl.ds(pl.multiple_of(me * rows, rows), rows)],
            x_local.at[target],
        )

    def dv_copy(g, offset, sender, device):
        place = dvt_all.at[cols(g), cols(sender, rows)]
        return remote(place, place, dv_send.at[g, offset - 1], dv_recv.at[g, offset - 1], device)

    def w_copy(g, source, target):
        here = cols(g)
        return remote(
            w_send.at[target, here], w_recv.at[source, here],
            ws_send.at[target, g], ws_recv.at[source, g], level(target),
        )

    table = target_orders(depth)

    def target_at(step):
        target = jnp.int32(0)
        for place in range(depth):
            for number in range(depth):
                here = ((z == place) & (step == number)).astype(jnp.int32)
                target = target + here * table[place][number]
        return target

    @pl.when(ctx == 0)
    def _():
        for g in range(KVH):
            for part in range(2):
                kv_copy(g, part).start()

    targets = [target_at(step) for step in range(depth)]
    for target in targets:
        for offset in range(2, PLANE, 2):
            other, device = peer(offset)
            x_copy(target, offset, me, other, device).start()
        own_copy(target).start()

    @pl.when(ctx == 0)
    def _():
        for g in range(KVH):
            for part in range(2):
                kv_copy(g, part).wait_send()

    for target in targets:
        for offset in range(1, PLANE, 2):
            other, device = peer(offset)
            x_copy(target, offset, me, other, device).start()

    for copy in inputs:
        copy.wait()

    shape = (2 * rows, rows)
    first = ctx * rows
    query_pos, query_docs = documents_of(len_ref, shape, 1, first)
    key_pos, key_docs = documents_of(len_ref, shape, 0, first - rows)
    allowed = (query_docs == key_docs) & (key_pos <= query_pos)
    bias[...] = jnp.where(allowed, 0.0, NEG_FILL)

    def attend(g, blocks):
        length = blocks * rows
        here = cols(g)
        key_part, value_part = k_ref[:, here], v_ref[:, here]
        if blocks == 2:
            key_part = jnp.concatenate([k_prev[:, here], key_part], axis=0)
            value_part = jnp.concatenate([v_prev[:, here], value_part], axis=0)
        key_turned = key_part.astype(F32).T.astype(BF16)
        key_sum = jnp.zeros((length, HD), F32)
        value_sum = jnp.zeros((length, HD), F32)
        mask = jnp.concatenate([bias[2 * rows - length:]] * PAIR, axis=1)
        for pair in range(GROUP // PAIR):
            heads = [cols(g * GROUP + pair * PAIR + i) for i in range(PAIR)]
            query = jnp.concatenate([q_ref[:, h] for h in heads], axis=0)
            grad = jnp.concatenate([go_ref[:, h] for h in heads], axis=0)
            scores = nt(key_part, query) * (scale * LOG2E) + mask
            top = jnp.max(scores, axis=0, keepdims=True)
            weight = jnp.exp2(scores - top)
            prob = weight * (1.0 / jnp.sum(weight, axis=0, keepdims=True))
            prob_low = prob.astype(BF16)
            dprob = nt(value_part, grad)
            delta = jnp.sum(prob_low.astype(F32) * dprob, axis=0, keepdims=True)
            dscore = (prob * (dprob - delta)).astype(BF16)
            value_sum = value_sum + nn(prob_low, grad)
            key_sum = key_sum + nn(dscore, query)
            turned = nn(key_turned, dscore) * scale
            for i, h in enumerate(heads):
                dq_ref[:, h] = turned[:, i * rows:(i + 1) * rows].T.astype(BF16)
        return key_sum * scale, value_sum

    def finish(g, key_sum, value_sum):
        here = cols(g)
        dk_ref[:, here] = key_sum.astype(BF16)
        dv_ref[:, here] = value_sum.astype(BF16)
        dvt_all[here, cols(me, rows)] = value_sum.T.astype(BF16)

    def shell(m):
        for offset in range(1, PLANE):
            sender = (me + PLANE - offset) % PLANE
            dv_copy(m, offset, sender, peer(offset)[1]).wait_recv()

        def block(i, carry):
            old = (i < m).astype(jnp.int32)
            step = old * i + (1 - old) * m
            g = old * m + (1 - old) * (i - m)
            target = target_at(step)

            @pl.when(i == m)
            def _():
                x_wait(target)

            product = nn(dvt_all[cols(g)], x_all[target])
            w_send[target, cols(g)] = product.astype(BF16)
            w_copy(g, z, target).start()
            return carry

        last = (m == depth - 1).astype(jnp.int32)
        lax.fori_loop(0, 2 * m + 1 - last * (m + 1), block, 0)

    def x_wait(target):
        for offset in range(1, PLANE):
            sender = (me + PLANE - offset) % PLANE
            x_copy(target, offset, sender, me, peer(offset)[1]).wait_recv()
        own_copy(target).wait()

    def group(g, carry):
        @pl.when(ctx == 0)
        def _():
            key_sum, value_sum = attend(g, 1)
            for part in range(2):
                term_copy(g, part).wait_recv()
            finish(g, key_sum + term_k[g].astype(F32), value_sum + term_v[g].astype(F32))

        @pl.when(ctx == 1)
        def _():
            for part in range(2):
                kv_copy(g, part).wait_recv()
            key_sum, value_sum = attend(g, 2)
            term_v[g] = value_sum[:rows].astype(BF16)
            term_k[g] = key_sum[:rows].astype(BF16)
            for part in range(2):
                term_copy(g, part).start()
            finish(g, key_sum[rows:], value_sum[rows:])

        for offset in range(1, PLANE):
            dv_copy(g, offset, me, peer(offset)[1]).start()

        @pl.when(g > 0)
        def _():
            shell(g - 1)

        return carry

    lax.fori_loop(0, KVH, group, 0)
    shell(jnp.int32(KVH - 1))
    x_wait(z)
    w_own[...] = nn(dvt_all[...], x_all[z])
    for step in range(1, depth):
        source = (z + step) % depth
        for g in range(KVH):
            w_copy(g, source, z).wait_recv()
        w_own[...] += w_recv[source].astype(F32)
    w_ref[...] = (w_own[...] * out_scale).T

    for target in targets:
        for offset in range(1, PLANE):
            other, device = peer(offset)
            x_copy(target, offset, me, other, device).wait_send()
    for step in range(1, depth):
        for g in range(KVH):
            w_copy(g, z, (z + step) % depth).wait_send()
    for g in range(KVH):
        for offset in range(1, PLANE):
            dv_copy(g, offset, me, peer(offset)[1]).wait_send()

    @pl.when(ctx == 1)
    def _():
        for g in range(KVH):
            for part in range(2):
                term_copy(g, part).wait_send()


def fused(query_heads, key_heads, value_heads, out_grad, layer_inputs, doc_lengths):
    rows, model = layer_inputs.shape[1:]
    key_width = key_heads.shape[2]
    count = lax.axis_size("dp") * lax.axis_size("ctx")
    depth = count // PLANE
    width = model // count
    out_scale = (lax.axis_size("dp") * lax.axis_size("ctx") * rows) ** (-0.5)
    vmem = pl.BlockSpec(memory_space=pltpu.VMEM)
    dma = pltpu.SemaphoreType.DMA
    query_grad, key_grad, value_grad, weight_grad = pl.pallas_call(
        functools.partial(kernel, depth, out_scale),
        out_shape=(
            jax.ShapeDtypeStruct(query_heads.shape[1:], BF16),
            jax.ShapeDtypeStruct((rows, key_width), BF16),
            jax.ShapeDtypeStruct((rows, key_width), BF16),
            jax.ShapeDtypeStruct((width, key_width), F32),
        ),
        in_specs=[pl.BlockSpec(memory_space=pl.ANY)] * 5 + [pl.BlockSpec(memory_space=pltpu.SMEM)],
        out_specs=(vmem,) * 4,
        scratch_shapes=[
            pltpu.VMEM(query_heads.shape[1:], BF16),
            pltpu.VMEM((rows, key_width), BF16),
            pltpu.VMEM((rows, key_width), BF16),
            pltpu.VMEM(query_heads.shape[1:], BF16),
            pltpu.VMEM((rows, key_width), BF16),
            pltpu.VMEM((rows, key_width), BF16),
            pltpu.VMEM((2 * rows, rows), F32),
            pltpu.VMEM((KVH, rows, HD), BF16),
            pltpu.VMEM((KVH, rows, HD), BF16),
            pltpu.VMEM((depth, PLANE * rows, width), BF16),
            pltpu.VMEM((key_width, PLANE * rows), BF16),
            pltpu.VMEM((depth, key_width, width), BF16),
            pltpu.VMEM((depth, key_width, width), BF16),
            pltpu.VMEM((key_width, width), F32),
            dma((4,)), dma((2, KVH)), dma((2, KVH)), dma((2, KVH)), dma((2, KVH)),
            dma((depth, PLANE - 1)), dma((depth, PLANE - 1)), dma((depth,)),
            dma((KVH, PLANE - 1)), dma((KVH, PLANE - 1)),
            dma((depth, KVH)), dma((depth, KVH)),
        ],
        compiler_params=pltpu.CompilerParams(
            collective_id=0, has_side_effects=True, vmem_limit_bytes=48 * 1024 * 1024
        ),
    )(query_heads[0], key_heads[0], value_heads[0], out_grad[0], layer_inputs[0], doc_lengths)
    return (query_grad[None], key_grad[None], value_grad[None], weight_grad)


def document_ids(lengths_row, length):
    endings = jnp.cumsum(lengths_row)
    positions = jnp.arange(length, dtype=jnp.int32)
    return jnp.sum((positions[:, None] >= endings[None, :]).astype(jnp.int32), axis=1)


def shards(query_heads, key_heads, value_heads, out_grad, layer_inputs, doc_lengths):
    queries_here = query_heads[0]
    rows_here = queries_here.shape[0]
    shard_count = lax.axis_size("ctx")
    data_count = lax.axis_size("dp")
    length = rows_here * shard_count
    group_size = HEADS // KVH
    softmax_scale = HD ** (-0.5)
    key_width = key_heads.shape[2]
    key_all, value_all = (
        lax.all_gather(key_heads[0], "ctx", axis=0, tiled=True),
        lax.all_gather(value_heads[0], "ctx", axis=0, tiled=True),
    )
    documents = document_ids(doc_lengths[0], length)
    first_row = lax.axis_index("ctx") * rows_here
    positions = jnp.arange(length, dtype=jnp.int32)
    query_pos = first_row + jnp.arange(rows_here, dtype=jnp.int32)
    query_docs = lax.dynamic_slice_in_dim(documents, first_row, rows_here)
    allowed = (query_docs[:, None] == documents[None, :]) & (
        positions[None, :] <= query_pos[:, None]
    )
    query_split = queries_here.reshape(rows_here, KVH, group_size, HD)
    key_split = key_all.reshape(length, KVH, HD)
    value_split = value_all.reshape(length, KVH, HD)
    grad_split = out_grad[0].reshape(rows_here, KVH, group_size, HD)
    scores = (
        jnp.einsum("igsd,jgd->gsij", query_split, key_split, preferred_element_type=jnp.float32)
        * softmax_scale
    )
    scores = jnp.where(allowed[None, None], scores, NEG_FILL)
    row_top = jnp.max(scores, axis=-1, keepdims=True)
    row_total = jnp.sum(jnp.exp(scores - row_top), axis=-1, keepdims=True)
    probability = jnp.exp(scores - (row_top + jnp.log(row_total)))
    prob_low = probability.astype(jnp.bfloat16)
    attended = jnp.einsum(
        "gsij,jgd->igsd", prob_low, value_split, preferred_element_type=jnp.float32
    )
    delta = jnp.transpose(jnp.sum(grad_split.astype(jnp.float32) * attended, axis=-1), (1, 2, 0))
    dprob = jnp.einsum(
        "igsd,jgd->gsij", grad_split, value_split, preferred_element_type=jnp.float32
    )
    dscore_low = (probability * (dprob - delta[..., None])).astype(jnp.bfloat16)
    query_grad = (
        jnp.einsum("gsij,jgd->igsd", dscore_low, key_split, preferred_element_type=jnp.float32)
        * softmax_scale
    )
    query_grad = query_grad.reshape(rows_here, HEADS * HD).astype(jnp.bfloat16)
    key_term = (
        jnp.einsum("gsij,igsd->jgd", dscore_low, query_split, preferred_element_type=jnp.float32)
        * softmax_scale
    )
    value_term = jnp.einsum(
        "gsij,igsd->jgd", prob_low, grad_split, preferred_element_type=jnp.float32
    )
    summed_grads = lax.psum_scatter(
        jnp.concatenate(
            [
                key_term.reshape(lax.axis_size("ctx") * rows_here, key_width),
                value_term.reshape(lax.axis_size("ctx") * rows_here, key_width),
            ],
            axis=1,
        ),
        "ctx",
        scatter_dimension=0,
        tiled=True,
    )
    key_grad = summed_grads[:, :key_width].astype(jnp.bfloat16)
    value_grad = summed_grads[:, key_width:].astype(jnp.bfloat16)
    inputs_here = layer_inputs[0]
    weight_grad = lax.psum_scatter(
        jnp.einsum("te,tc->ec", inputs_here, value_grad, preferred_element_type=jnp.float32),
        ("dp", "ctx"),
        scatter_dimension=0,
        tiled=True,
    )
    weight_grad = weight_grad * (data_count * length) ** (-0.5)
    return (query_grad[None], key_grad[None], value_grad[None], weight_grad)


def place(query_heads, key_heads, value_heads, out_grad, layer_inputs, doc_lengths):
    arrays = (query_heads, key_heads, value_heads, out_grad, layer_inputs, doc_lengths)
    rows, model = layer_inputs.shape[1:]
    count = lax.axis_size("dp") * lax.axis_size("ctx")
    whole_tiles = rows % HD == 0 and model % (count * HD) == 0
    if lax.axis_size("ctx") == 2 and count == PLANE * KVH and whole_tiles:
        return fused(*arrays)
    return shards(*arrays)


def solution(mesh):
    placed = (
        P("dp", "ctx", None),
        P("dp", "ctx", None),
        P("dp", "ctx", None),
        P("dp", "ctx", None),
        P("dp", "ctx", None),
        P("dp", None),
    )
    return jax.shard_map(
        place,
        mesh=mesh,
        in_specs=placed,
        out_specs=(
            P("dp", "ctx", None),
            P("dp", "ctx", None),
            P("dp", "ctx", None),
            P(("dp", "ctx"), None),
        ),
        check_vma=False,
    )
```

```python
import functools
import math

import jax
import jax.numpy as jnp
from jax import lax
from jax.experimental import pallas as pl
from jax.experimental.pallas import tpu as pltpu
from jax.sharding import PartitionSpec as P

HD = 128
HEADS = 32
KVH = 4
GROUP = HEADS // KVH
PAIR = 2
PLANE = 8
LOG2E = math.log2(math.e)
F32 = jnp.float32
BF16 = jnp.bfloat16
MESH = pl.DeviceIdType.MESH


NEG_FILL = -1e30


def nt(a, b):
    return lax.dot_general(a, b, (((1,), (1,)), ((), ())), preferred_element_type=F32)


def nn(a, b):
    return jnp.dot(a, b, preferred_element_type=F32)


def cols(index, width=HD):
    return pl.ds(pl.multiple_of(index * width, width), width)


def target_orders(depth):
    table = []
    for z in range(depth):
        others = [t for t in range(depth) if t != z]
        others.sort(key=lambda t: (-abs(t - z), t))
        table.append(others + [z])
    return table


def documents_of(lengths, shape, axis, first):
    positions = lax.broadcasted_iota(jnp.int32, shape, axis) + first
    found = jnp.zeros(shape, jnp.int32)
    ending = jnp.int32(0)
    for number in range(lengths.shape[1]):
        ending = ending + lengths[0, number]
        found = found + (positions >= ending).astype(jnp.int32)
    return positions, found


def kernel(
    depth, out_scale,
    q_hbm, k_hbm, v_hbm, go_hbm, x_ref, len_ref,
    dq_ref, dk_ref, dv_ref, w_ref,
    q_ref, k_ref, v_ref, go_ref, k_prev, v_prev, bias, term_k, term_v,
    x_pack, x_all, dvt_all, w_send, w_recv, w_own,
    in_sem, kv_send, kv_recv, term_send, term_recv,
    x_send, x_recv, x_local, dv_send, dv_recv, ws_send, ws_recv,
):
    rows = q_ref.shape[0]
    dp = lax.axis_index("dp")
    ctx = lax.axis_index("ctx")
    lanes = PLANE // 2
    z = dp // lanes
    lane = dp % lanes
    me = lane * 2 + ctx
    width = w_ref.shape[0]
    scale = HD ** -0.5

    table = target_orders(depth)

    def target_at(step):
        target = jnp.int32(0)
        for place in range(depth):
            for number in range(depth):
                here = ((z == place) & (step == number)).astype(jnp.int32)
                target = target + here * table[place][number]
        return target

    targets = [target_at(step) for step in range(depth)]

    def pack_copy(target, offset):
        own = x_all.at[target, pl.ds(pl.multiple_of(me * rows, rows), rows)]
        return pltpu.make_async_copy(
            x_ref.at[:, cols(target * PLANE + (me + offset) % PLANE, width)],
            x_pack.at[target, offset] if offset else own,
            x_local.at[target, offset],
        )

    inputs = [
        pltpu.make_async_copy(src, dst, in_sem.at[i])
        for i, (src, dst) in enumerate(
            [(k_hbm, k_ref), (v_hbm, v_ref), (q_hbm, q_ref), (go_hbm, go_ref)]
        )
    ]
    for target in targets:
        for offset in [*range(2, PLANE, 2), *range(1, PLANE, 2), 0]:
            pack_copy(target, offset).start()
    for copy in inputs:
        copy.start()

    def peer(offset):
        other = (me + offset) % PLANE
        return other, (z * lanes + other // 2, other % 2)

    def level(target):
        return (target * lanes + lane, ctx)

    partner = (dp, 1 - ctx)

    barrier = pltpu.get_barrier_semaphore()
    for offset in range(1, PLANE):
        pl.semaphore_signal(barrier, inc=1, device_id=peer(offset)[1], device_id_type=MESH)
    for step in range(1, depth):
        pl.semaphore_signal(barrier, inc=1, device_id=level((z + step) % depth), device_id_type=MESH)
    pl.semaphore_wait(barrier, PLANE - 1 + depth - 1)

    def remote(src, dst, send, recv, device):
        return pltpu.make_async_remote_copy(
            src_ref=src, dst_ref=dst, send_sem=send, recv_sem=recv,
            device_id=device, device_id_type=MESH,
        )

    def kv_copy(g, part):
        src, dst = ((k_hbm, k_prev), (v_hbm, v_prev))[part]
        here = cols(g)
        return remote(src.at[:, here], dst.at[:, here], kv_send.at[part, g], kv_recv.at[part, g], partner)

    def term_copy(g, part):
        buffer = (term_v, term_k)[part].at[g]
        return remote(buffer, buffer, term_send.at[part, g], term_recv.at[part, g], partner)

    def x_copy(target, offset, sender, device):
        return remote(
            x_pack.at[target, offset],
            x_all.at[target, pl.ds(pl.multiple_of(sender * rows, rows), rows)],
            x_send.at[target, offset - 1], x_recv.at[target, offset - 1], device,
        )

    def dv_copy(g, offset, sender, device):
        place = dvt_all.at[g, sender]
        return remote(place, place, dv_send.at[g, offset - 1], dv_recv.at[g, offset - 1], device)

    def w_copy(g, source, target):
        here = cols(g)
        return remote(
            w_send.at[target, here], w_recv.at[source, here],
            ws_send.at[target, g], ws_recv.at[source, g], level(target),
        )

    @pl.when(ctx == 0)
    def _():
        for g in range(KVH):
            for part in range(2):
                kv_copy(g, part).start()

    for target in targets:
        for offset in range(2, PLANE, 2):
            pack_copy(target, offset).wait()
            x_copy(target, offset, me, peer(offset)[1]).start()

    @pl.when(ctx == 0)
    def _():
        for g in range(KVH):
            for part in range(2):
                kv_copy(g, part).wait_send()

    for target in targets:
        for offset in range(1, PLANE, 2):
            pack_copy(target, offset).wait()
            x_copy(target, offset, me, peer(offset)[1]).start()

    for copy in inputs:
        copy.wait()

    shape = (2 * rows, rows)
    first = ctx * rows
    query_pos, query_docs = documents_of(len_ref, shape, 1, first)
    key_pos, key_docs = documents_of(len_ref, shape, 0, first - rows)
    allowed = (query_docs == key_docs) & (key_pos <= query_pos)
    bias[...] = jnp.where(allowed, 0.0, NEG_FILL)

    def attend(g, blocks):
        length = blocks * rows
        here = cols(g)
        key_part, value_part = k_ref[:, here], v_ref[:, here]
        if blocks == 2:
            key_part = jnp.concatenate([k_prev[:, here], key_part], axis=0)
            value_part = jnp.concatenate([v_prev[:, here], value_part], axis=0)
        key_turned = key_part.astype(F32).T.astype(BF16)
        key_sum = jnp.zeros((length, HD), F32)
        value_sum = jnp.zeros((length, HD), F32)
        mask = jnp.concatenate([bias[2 * rows - length:]] * PAIR, axis=1)
        for pair in range(GROUP // PAIR):
            heads = [cols(g * GROUP + pair * PAIR + i) for i in range(PAIR)]
            query = jnp.concatenate([q_ref[:, h] for h in heads], axis=0)
            grad = jnp.concatenate([go_ref[:, h] for h in heads], axis=0)
            scores = nt(key_part, query) * (scale * LOG2E) + mask
            top = jnp.max(scores, axis=0, keepdims=True)
            weight = jnp.exp2(scores - top)
            prob = weight * (1.0 / jnp.sum(weight, axis=0, keepdims=True))
            prob_low = prob.astype(BF16)
            dprob = nt(value_part, grad)
            delta = jnp.sum(prob_low.astype(F32) * dprob, axis=0, keepdims=True)
            dscore = (prob * (dprob - delta)).astype(BF16)
            value_sum = value_sum + nn(prob_low, grad)
            key_sum = key_sum + nn(dscore, query)
            turned = nn(key_turned, dscore) * scale
            for i, h in enumerate(heads):
                dq_ref[:, h] = turned[:, i * rows:(i + 1) * rows].T.astype(BF16)
        return key_sum * scale, value_sum

    def finish(g, key_sum, value_sum):
        here = cols(g)
        dk_ref[:, here] = key_sum.astype(BF16)
        dv_ref[:, here] = value_sum.astype(BF16)
        dvt_all[g, me] = value_sum.T.astype(BF16)

    def gathered(g):
        return jnp.concatenate([dvt_all[g, sender] for sender in range(PLANE)], axis=1)

    def shell(m):
        for offset in range(1, PLANE):
            sender = (me + PLANE - offset) % PLANE
            dv_copy(m, offset, sender, peer(offset)[1]).wait_recv()

        def block(i, carry):
            old = (i < m).astype(jnp.int32)
            step = old * i + (1 - old) * m
            g = old * m + (1 - old) * (i - m)
            target = target_at(step)

            @pl.when(i == m)
            def _():
                x_wait(target)

            product = nn(gathered(g), x_all[target])
            w_send[target, cols(g)] = product.astype(BF16)
            w_copy(g, z, target).start()
            return carry

        last = (m == depth - 1).astype(jnp.int32)
        lax.fori_loop(0, 2 * m + 1 - last * (m + 1), block, 0)

    def x_wait(target):
        for offset in range(1, PLANE):
            sender = (me + PLANE - offset) % PLANE
            x_copy(target, offset, sender, peer(offset)[1]).wait_recv()
        pack_copy(target, 0).wait()

    def group(g, carry):
        @pl.when(ctx == 0)
        def _():
            key_sum, value_sum = attend(g, 1)
            for part in range(2):
                term_copy(g, part).wait_recv()
            finish(g, key_sum + term_k[g].astype(F32), value_sum + term_v[g].astype(F32))

        @pl.when(ctx == 1)
        def _():
            for part in range(2):
                kv_copy(g, part).wait_recv()
            key_sum, value_sum = attend(g, 2)
            term_v[g] = value_sum[:rows].astype(BF16)
            term_k[g] = key_sum[:rows].astype(BF16)
            for part in range(2):
                term_copy(g, part).start()
            finish(g, key_sum[rows:], value_sum[rows:])

        for offset in range(1, PLANE):
            dv_copy(g, offset, me, peer(offset)[1]).start()

        @pl.when(g > 0)
        def _():
            shell(g - 1)

        return carry

    lax.fori_loop(0, KVH, group, 0)
    shell(jnp.int32(KVH - 1))
    x_wait(z)
    w_own[...] = nn(jnp.concatenate([gathered(g) for g in range(KVH)], axis=0), x_all[z])
    for step in range(1, depth):
        source = (z + step) % depth
        for g in range(KVH):
            w_copy(g, source, z).wait_recv()
        w_own[...] += w_recv[source].astype(F32)
    w_ref[...] = (w_own[...] * out_scale).T

    for target in targets:
        for offset in range(1, PLANE):
            x_copy(target, offset, me, peer(offset)[1]).wait_send()
    for step in range(1, depth):
        for g in range(KVH):
            w_copy(g, z, (z + step) % depth).wait_send()
    for g in range(KVH):
        for offset in range(1, PLANE):
            dv_copy(g, offset, me, peer(offset)[1]).wait_send()

    @pl.when(ctx == 1)
    def _():
        for g in range(KVH):
            for part in range(2):
                term_copy(g, part).wait_send()


def fused(query_heads, key_heads, value_heads, out_grad, layer_inputs, doc_lengths):
    rows, model = layer_inputs.shape[1:]
    key_width = key_heads.shape[2]
    count = lax.axis_size("dp") * lax.axis_size("ctx")
    depth = count // PLANE
    width = model // count
    out_scale = (lax.axis_size("dp") * lax.axis_size("ctx") * rows) ** (-0.5)
    vmem = pl.BlockSpec(memory_space=pltpu.VMEM)
    dma = pltpu.SemaphoreType.DMA
    query_grad, key_grad, value_grad, weight_grad = pl.pallas_call(
        functools.partial(kernel, depth, out_scale),
        out_shape=(
            jax.ShapeDtypeStruct(query_heads.shape[1:], BF16),
            jax.ShapeDtypeStruct((rows, key_width), BF16),
            jax.ShapeDtypeStruct((rows, key_width), BF16),
            jax.ShapeDtypeStruct((width, key_width), F32),
        ),
        in_specs=[pl.BlockSpec(memory_space=pltpu.HBM)] * 5 + [pl.BlockSpec(memory_space=pltpu.SMEM)],
        out_specs=(vmem,) * 4,
        scratch_shapes=[
            pltpu.VMEM(query_heads.shape[1:], BF16),
            pltpu.VMEM((rows, key_width), BF16),
            pltpu.VMEM((rows, key_width), BF16),
            pltpu.VMEM(query_heads.shape[1:], BF16),
            pltpu.VMEM((rows, key_width), BF16),
            pltpu.VMEM((rows, key_width), BF16),
            pltpu.VMEM((2 * rows, rows), F32),
            pltpu.VMEM((KVH, rows, HD), BF16),
            pltpu.VMEM((KVH, rows, HD), BF16),
            pltpu.VMEM((depth, PLANE, rows, width), BF16),
            pltpu.VMEM((depth, PLANE * rows, width), BF16),
            pltpu.VMEM((KVH, PLANE, HD, rows), BF16),
            pltpu.VMEM((depth, key_width, width), BF16),
            pltpu.VMEM((depth, key_width, width), BF16),
            pltpu.VMEM((key_width, width), F32),
            dma((4,)), dma((2, KVH)), dma((2, KVH)), dma((2, KVH)), dma((2, KVH)),
            dma((depth, PLANE - 1)), dma((depth, PLANE - 1)), dma((depth, PLANE)),
            dma((KVH, PLANE - 1)), dma((KVH, PLANE - 1)),
            dma((depth, KVH)), dma((depth, KVH)),
        ],
        compiler_params=pltpu.CompilerParams(
            collective_id=0, has_side_effects=True, vmem_limit_bytes=64 * 1024 * 1024
        ),
    )(query_heads[0], key_heads[0], value_heads[0], out_grad[0], layer_inputs[0], doc_lengths)
    return (query_grad[None], key_grad[None], value_grad[None], weight_grad)


def document_ids(lengths_row, length):
    endings = jnp.cumsum(lengths_row)
    positions = jnp.arange(length, dtype=jnp.int32)
    return jnp.sum((positions[:, None] >= endings[None, :]).astype(jnp.int32), axis=1)


def shards(query_heads, key_heads, value_heads, out_grad, layer_inputs, doc_lengths):
    queries_here = query_heads[0]
    rows_here = queries_here.shape[0]
    shard_count = lax.axis_size("ctx")
    data_count = lax.axis_size("dp")
    length = rows_here * shard_count
    group_size = HEADS // KVH
    softmax_scale = HD ** (-0.5)
    key_width = key_heads.shape[2]
    key_all, value_all = (
        lax.all_gather(key_heads[0], "ctx", axis=0, tiled=True),
        lax.all_gather(value_heads[0], "ctx", axis=0, tiled=True),
    )
    documents = document_ids(doc_lengths[0], length)
    first_row = lax.axis_index("ctx") * rows_here
    positions = jnp.arange(length, dtype=jnp.int32)
    query_pos = first_row + jnp.arange(rows_here, dtype=jnp.int32)
    query_docs = lax.dynamic_slice_in_dim(documents, first_row, rows_here)
    allowed = (query_docs[:, None] == documents[None, :]) & (
        positions[None, :] <= query_pos[:, None]
    )
    query_split = queries_here.reshape(rows_here, KVH, group_size, HD)
    key_split = key_all.reshape(length, KVH, HD)
    value_split = value_all.reshape(length, KVH, HD)
    grad_split = out_grad[0].reshape(rows_here, KVH, group_size, HD)
    scores = (
        jnp.einsum("igsd,jgd->gsij", query_split, key_split, preferred_element_type=jnp.float32)
        * softmax_scale
    )
    scores = jnp.where(allowed[None, None], scores, NEG_FILL)
    row_top = jnp.max(scores, axis=-1, keepdims=True)
    row_total = jnp.sum(jnp.exp(scores - row_top), axis=-1, keepdims=True)
    probability = jnp.exp(scores - (row_top + jnp.log(row_total)))
    prob_low = probability.astype(jnp.bfloat16)
    attended = jnp.einsum(
        "gsij,jgd->igsd", prob_low, value_split, preferred_element_type=jnp.float32
    )
    delta = jnp.transpose(jnp.sum(grad_split.astype(jnp.float32) * attended, axis=-1), (1, 2, 0))
    dprob = jnp.einsum(
        "igsd,jgd->gsij", grad_split, value_split, preferred_element_type=jnp.float32
    )
    dscore_low = (probability * (dprob - delta[..., None])).astype(jnp.bfloat16)
    query_grad = (
        jnp.einsum("gsij,jgd->igsd", dscore_low, key_split, preferred_element_type=jnp.float32)
        * softmax_scale
    )
    query_grad = query_grad.reshape(rows_here, HEADS * HD).astype(jnp.bfloat16)
    key_term = (
        jnp.einsum("gsij,igsd->jgd", dscore_low, query_split, preferred_element_type=jnp.float32)
        * softmax_scale
    )
    value_term = jnp.einsum(
        "gsij,igsd->jgd", prob_low, grad_split, preferred_element_type=jnp.float32
    )
    summed_grads = lax.psum_scatter(
        jnp.concatenate(
            [
                key_term.reshape(lax.axis_size("ctx") * rows_here, key_width),
                value_term.reshape(lax.axis_size("ctx") * rows_here, key_width),
            ],
            axis=1,
        ),
        "ctx",
        scatter_dimension=0,
        tiled=True,
    )
    key_grad = summed_grads[:, :key_width].astype(jnp.bfloat16)
    value_grad = summed_grads[:, key_width:].astype(jnp.bfloat16)
    inputs_here = layer_inputs[0]
    weight_grad = lax.psum_scatter(
        jnp.einsum("te,tc->ec", inputs_here, value_grad, preferred_element_type=jnp.float32),
        ("dp", "ctx"),
        scatter_dimension=0,
        tiled=True,
    )
    weight_grad = weight_grad * (data_count * length) ** (-0.5)
    return (query_grad[None], key_grad[None], value_grad[None], weight_grad)


def place(query_heads, key_heads, value_heads, out_grad, layer_inputs, doc_lengths):
    arrays = (query_heads, key_heads, value_heads, out_grad, layer_inputs, doc_lengths)
    rows, model = layer_inputs.shape[1:]
    count = lax.axis_size("dp") * lax.axis_size("ctx")
    whole_tiles = rows % HD == 0 and model % (count * HD) == 0
    if lax.axis_size("ctx") == 2 and count == PLANE * KVH and whole_tiles:
        return fused(*arrays)
    return shards(*arrays)


def solution(mesh):
    placed = (
        P("dp", "ctx", None),
        P("dp", "ctx", None),
        P("dp", "ctx", None),
        P("dp", "ctx", None),
        P("dp", "ctx", None),
        P("dp", None),
    )
    return jax.shard_map(
        place,
        mesh=mesh,
        in_specs=placed,
        out_specs=(
            P("dp", "ctx", None),
            P("dp", "ctx", None),
            P("dp", "ctx", None),
            P(("dp", "ctx"), None),
        ),
        check_vma=False,
    )
```

```python
import functools
import math

import jax
import jax.numpy as jnp
from jax import lax
from jax.experimental import pallas as pl
from jax.experimental.pallas import tpu as pltpu
from jax.sharding import PartitionSpec as P

HD = 128
HEADS = 32
KVH = 4
GROUP = HEADS // KVH
PAIR = 2
PLANE = 8
LOG2E = math.log2(math.e)
F32 = jnp.float32
BF16 = jnp.bfloat16
MESH = pl.DeviceIdType.MESH


NEG_FILL = -1e30


def nt(a, b):
    return lax.dot_general(a, b, (((1,), (1,)), ((), ())), preferred_element_type=F32)


def nn(a, b):
    return jnp.dot(a, b, preferred_element_type=F32)


def cols(index, width=HD):
    return pl.ds(pl.multiple_of(index * width, width), width)


def target_orders(depth):
    table = []
    for z in range(depth):
        others = [t for t in range(depth) if t != z]
        others.sort(key=lambda t: (-abs(t - z), t))
        table.append(others + [z])
    return table


def documents_of(lengths, shape, axis, first):
    positions = lax.broadcasted_iota(jnp.int32, shape, axis) + first
    found = jnp.zeros(shape, jnp.int32)
    ending = jnp.int32(0)
    for number in range(lengths.shape[1]):
        ending = ending + lengths[0, number]
        found = found + (positions >= ending).astype(jnp.int32)
    return positions, found


def kernel(
    depth, out_scale,
    q_hbm, k_hbm, v_hbm, go_hbm, x_ref, len_ref,
    dq_ref, dk_ref, dv_ref, w_ref,
    q_ref, k_ref, v_ref, go_ref, k_prev, v_prev, bias, term_k, term_v,
    x_pack, x_all, dvt_all, w_send, w_recv, w_own,
    in_sem, kv_send, kv_recv, term_send, term_recv,
    x_send, x_recv, x_local, dv_send, dv_recv, ws_send, ws_recv,
):
    rows = q_ref.shape[0]
    dp = lax.axis_index("dp")
    ctx = lax.axis_index("ctx")
    lanes = PLANE // 2
    z = dp // lanes
    lane = dp % lanes
    me = lane * 2 + ctx
    width = w_ref.shape[0]
    scale = HD ** -0.5

    table = target_orders(depth)

    def target_at(step):
        target = jnp.int32(0)
        for place in range(depth):
            for number in range(depth):
                here = ((z == place) & (step == number)).astype(jnp.int32)
                target = target + here * table[place][number]
        return target

    targets = [target_at(step) for step in range(depth)]

    def pack_copy(target, offset):
        own = x_all.at[target, pl.ds(pl.multiple_of(me * rows, rows), rows)]
        return pltpu.make_async_copy(
            x_ref.at[:, cols(target * PLANE + (me + offset) % PLANE, width)],
            x_pack.at[target, offset] if offset else own,
            x_local.at[target, offset],
        )

    inputs = [
        pltpu.make_async_copy(src, dst, in_sem.at[i])
        for i, (src, dst) in enumerate(
            [(k_hbm, k_ref), (v_hbm, v_ref), (q_hbm, q_ref), (go_hbm, go_ref)]
        )
    ]
    for target in targets:
        for offset in [*range(2, PLANE, 2), *range(1, PLANE, 2), 0]:
            pack_copy(target, offset).start()
    for copy in inputs:
        copy.start()

    def peer(offset):
        other = (me + offset) % PLANE
        return other, (z * lanes + other // 2, other % 2)

    def level(target):
        return (target * lanes + lane, ctx)

    partner = (dp, 1 - ctx)

    barrier = pltpu.get_barrier_semaphore()
    for offset in range(1, PLANE):
        pl.semaphore_signal(barrier, inc=1, device_id=peer(offset)[1], device_id_type=MESH)
    for step in range(1, depth):
        pl.semaphore_signal(barrier, inc=1, device_id=level((z + step) % depth), device_id_type=MESH)
    pl.semaphore_wait(barrier, PLANE - 1 + depth - 1)

    def remote(src, dst, send, recv, device):
        return pltpu.make_async_remote_copy(
            src_ref=src, dst_ref=dst, send_sem=send, recv_sem=recv,
            device_id=device, device_id_type=MESH,
        )

    def kv_copy(g, part):
        src, dst = ((k_hbm, k_prev), (v_hbm, v_prev))[part]
        here = cols(g)
        return remote(src.at[:, here], dst.at[:, here], kv_send.at[part, g], kv_recv.at[part, g], partner)

    def term_copy(g, part):
        buffer = (term_v, term_k)[part].at[g]
        return remote(buffer, buffer, term_send.at[part, g], term_recv.at[part, g], partner)

    def x_copy(target, offset, sender, device):
        return remote(
            x_pack.at[target, offset],
            x_all.at[target, pl.ds(pl.multiple_of(sender * rows, rows), rows)],
            x_send.at[target, offset - 1], x_recv.at[target, offset - 1], device,
        )

    def dv_copy(g, offset, sender, device):
        place = dvt_all.at[g, sender]
        return remote(place, place, dv_send.at[g, offset - 1], dv_recv.at[g, offset - 1], device)

    def w_copy(g, source, target):
        here = cols(g)
        return remote(
            w_send.at[target, here], w_recv.at[source, here],
            ws_send.at[target, g], ws_recv.at[source, g], level(target),
        )

    @pl.when(ctx == 0)
    def _():
        for g in range(KVH):
            for part in range(2):
                kv_copy(g, part).start()

    def x_start(step, offset):
        x_copy(target_at(step), offset, me, peer(offset)[1]).start()

    def x_packed(step):
        for offset in range(1, PLANE):
            pack_copy(targets[step], offset).wait()

    x_packed(0)
    for offset in range(2, PLANE, 2):
        x_start(0, offset)

    @pl.when(ctx == 0)
    def _():
        for g in range(KVH):
            for part in range(2):
                kv_copy(g, part).wait_send()

    for offset in range(1, PLANE, 2):
        x_start(0, offset)
    for step in range(1, depth):
        x_packed(step)

    for copy in inputs:
        copy.wait()

    shape = (2 * rows, rows)
    first = ctx * rows
    query_pos, query_docs = documents_of(len_ref, shape, 1, first)
    key_pos, key_docs = documents_of(len_ref, shape, 0, first - rows)
    allowed = (query_docs == key_docs) & (key_pos <= query_pos)
    bias[...] = jnp.where(allowed, 0.0, NEG_FILL)

    def attend(g, blocks):
        length = blocks * rows
        here = cols(g)
        key_part, value_part = k_ref[:, here], v_ref[:, here]
        if blocks == 2:
            key_part = jnp.concatenate([k_prev[:, here], key_part], axis=0)
            value_part = jnp.concatenate([v_prev[:, here], value_part], axis=0)
        key_turned = key_part.astype(F32).T.astype(BF16)
        key_sum = jnp.zeros((length, HD), F32)
        value_sum = jnp.zeros((length, HD), F32)
        mask = jnp.concatenate([bias[2 * rows - length:]] * PAIR, axis=1)
        for pair in range(GROUP // PAIR):
            heads = [cols(g * GROUP + pair * PAIR + i) for i in range(PAIR)]
            query = jnp.concatenate([q_ref[:, h] for h in heads], axis=0)
            grad = jnp.concatenate([go_ref[:, h] for h in heads], axis=0)
            scores = nt(key_part, query) * (scale * LOG2E) + mask
            top = jnp.max(scores, axis=0, keepdims=True)
            weight = jnp.exp2(scores - top)
            prob = weight * (1.0 / jnp.sum(weight, axis=0, keepdims=True))
            prob_low = prob.astype(BF16)
            dprob = nt(value_part, grad)
            delta = jnp.sum(prob_low.astype(F32) * dprob, axis=0, keepdims=True)
            dscore = (prob * (dprob - delta)).astype(BF16)
            value_sum = value_sum + nn(prob_low, grad)
            key_sum = key_sum + nn(dscore, query)
            turned = nn(key_turned, dscore) * scale
            for i, h in enumerate(heads):
                dq_ref[:, h] = turned[:, i * rows:(i + 1) * rows].T.astype(BF16)
        return key_sum * scale, value_sum

    def finish(g, key_sum, value_sum):
        here = cols(g)
        dk_ref[:, here] = key_sum.astype(BF16)
        dv_ref[:, here] = value_sum.astype(BF16)
        dvt_all[g, me] = value_sum.T.astype(BF16)

    def gathered(g):
        return jnp.concatenate([dvt_all[g, sender] for sender in range(PLANE)], axis=1)

    def gather_wait(g):
        for offset in range(1, PLANE):
            sender = (me + PLANE - offset) % PLANE
            dv_copy(g, offset, sender, peer(offset)[1]).wait_recv()

    def first_block(g):
        gather_wait(g)
        target = targets[0]
        w_send[target, cols(g)] = nn(gathered(g), x_all[target]).astype(BF16)
        w_copy(g, z, target).start()

    def x_wait(target):
        for offset in range(1, PLANE):
            sender = (me + PLANE - offset) % PLANE
            x_copy(target, offset, sender, peer(offset)[1]).wait_recv()
        pack_copy(target, 0).wait()

    def group(g, carry):
        x_start(1, 2 * g + 1)

        @pl.when(2 * g + 2 < PLANE)
        def _():
            x_start(1, 2 * g + 2)

        @pl.when(ctx == 0)
        def _():
            key_sum, value_sum = attend(g, 1)
            for part in range(2):
                term_copy(g, part).wait_recv()
            finish(g, key_sum + term_k[g].astype(F32), value_sum + term_v[g].astype(F32))

        @pl.when(ctx == 1)
        def _():
            for part in range(2):
                kv_copy(g, part).wait_recv()
            key_sum, value_sum = attend(g, 2)
            term_v[g] = value_sum[:rows].astype(BF16)
            term_k[g] = key_sum[:rows].astype(BF16)
            for part in range(2):
                term_copy(g, part).start()
            finish(g, key_sum[rows:], value_sum[rows:])

        for offset in range(1, PLANE):
            dv_copy(g, offset, me, peer(offset)[1]).start()

        @pl.when(g == 1)
        def _():
            x_wait(targets[0])

        @pl.when(g > 0)
        def _():
            first_block(g - 1)

        return carry

    lax.fori_loop(0, KVH, group, 0)
    for step in range(2, depth):
        for offset in range(1, PLANE):
            x_start(step, offset)
    first_block(KVH - 1)

    def later(step, carry):
        target = target_at(step)
        x_wait(target)
        spread = jnp.concatenate([gathered(g) for g in range(KVH)], axis=0)
        w_send[target] = nn(spread, x_all[target]).astype(BF16)
        for g in range(KVH):
            w_copy(g, z, target).start()
        return carry

    lax.fori_loop(1, depth - 1, later, 0)
    x_wait(z)
    w_own[...] = nn(jnp.concatenate([gathered(g) for g in range(KVH)], axis=0), x_all[z])
    for step in range(1, depth):
        source = (z + step) % depth
        for g in range(KVH):
            w_copy(g, source, z).wait_recv()
        w_own[...] += w_recv[source].astype(F32)
    w_ref[...] = (w_own[...] * out_scale).T

    for target in targets:
        for offset in range(1, PLANE):
            x_copy(target, offset, me, peer(offset)[1]).wait_send()
    for step in range(1, depth):
        for g in range(KVH):
            w_copy(g, z, (z + step) % depth).wait_send()
    for g in range(KVH):
        for offset in range(1, PLANE):
            dv_copy(g, offset, me, peer(offset)[1]).wait_send()

    @pl.when(ctx == 1)
    def _():
        for g in range(KVH):
            for part in range(2):
                term_copy(g, part).wait_send()


def fused(query_heads, key_heads, value_heads, out_grad, layer_inputs, doc_lengths):
    rows, model = layer_inputs.shape[1:]
    key_width = key_heads.shape[2]
    count = lax.axis_size("dp") * lax.axis_size("ctx")
    depth = count // PLANE
    width = model // count
    out_scale = (lax.axis_size("dp") * lax.axis_size("ctx") * rows) ** (-0.5)
    vmem = pl.BlockSpec(memory_space=pltpu.VMEM)
    dma = pltpu.SemaphoreType.DMA
    query_grad, key_grad, value_grad, weight_grad = pl.pallas_call(
        functools.partial(kernel, depth, out_scale),
        out_shape=(
            jax.ShapeDtypeStruct(query_heads.shape[1:], BF16),
            jax.ShapeDtypeStruct((rows, key_width), BF16),
            jax.ShapeDtypeStruct((rows, key_width), BF16),
            jax.ShapeDtypeStruct((width, key_width), F32),
        ),
        in_specs=[pl.BlockSpec(memory_space=pltpu.HBM)] * 5 + [pl.BlockSpec(memory_space=pltpu.SMEM)],
        out_specs=(vmem,) * 4,
        scratch_shapes=[
            pltpu.VMEM(query_heads.shape[1:], BF16),
            pltpu.VMEM((rows, key_width), BF16),
            pltpu.VMEM((rows, key_width), BF16),
            pltpu.VMEM(query_heads.shape[1:], BF16),
            pltpu.VMEM((rows, key_width), BF16),
            pltpu.VMEM((rows, key_width), BF16),
            pltpu.VMEM((2 * rows, rows), F32),
            pltpu.VMEM((KVH, rows, HD), BF16),
            pltpu.VMEM((KVH, rows, HD), BF16),
            pltpu.VMEM((depth, PLANE, rows, width), BF16),
            pltpu.VMEM((depth, PLANE * rows, width), BF16),
            pltpu.VMEM((KVH, PLANE, HD, rows), BF16),
            pltpu.VMEM((depth, key_width, width), BF16),
            pltpu.VMEM((depth, key_width, width), BF16),
            pltpu.VMEM((key_width, width), F32),
            dma((4,)), dma((2, KVH)), dma((2, KVH)), dma((2, KVH)), dma((2, KVH)),
            dma((depth, PLANE - 1)), dma((depth, PLANE - 1)), dma((depth, PLANE)),
            dma((KVH, PLANE - 1)), dma((KVH, PLANE - 1)),
            dma((depth, KVH)), dma((depth, KVH)),
        ],
        compiler_params=pltpu.CompilerParams(
            collective_id=0, has_side_effects=True, vmem_limit_bytes=64 * 1024 * 1024
        ),
    )(query_heads[0], key_heads[0], value_heads[0], out_grad[0], layer_inputs[0], doc_lengths)
    return (query_grad[None], key_grad[None], value_grad[None], weight_grad)


def document_ids(lengths_row, length):
    endings = jnp.cumsum(lengths_row)
    positions = jnp.arange(length, dtype=jnp.int32)
    return jnp.sum((positions[:, None] >= endings[None, :]).astype(jnp.int32), axis=1)


def shards(query_heads, key_heads, value_heads, out_grad, layer_inputs, doc_lengths):
    queries_here = query_heads[0]
    rows_here = queries_here.shape[0]
    shard_count = lax.axis_size("ctx")
    data_count = lax.axis_size("dp")
    length = rows_here * shard_count
    group_size = HEADS // KVH
    softmax_scale = HD ** (-0.5)
    key_width = key_heads.shape[2]
    key_all, value_all = (
        lax.all_gather(key_heads[0], "ctx", axis=0, tiled=True),
        lax.all_gather(value_heads[0], "ctx", axis=0, tiled=True),
    )
    documents = document_ids(doc_lengths[0], length)
    first_row = lax.axis_index("ctx") * rows_here
    positions = jnp.arange(length, dtype=jnp.int32)
    query_pos = first_row + jnp.arange(rows_here, dtype=jnp.int32)
    query_docs = lax.dynamic_slice_in_dim(documents, first_row, rows_here)
    allowed = (query_docs[:, None] == documents[None, :]) & (
        positions[None, :] <= query_pos[:, None]
    )
    query_split = queries_here.reshape(rows_here, KVH, group_size, HD)
    key_split = key_all.reshape(length, KVH, HD)
    value_split = value_all.reshape(length, KVH, HD)
    grad_split = out_grad[0].reshape(rows_here, KVH, group_size, HD)
    scores = (
        jnp.einsum("igsd,jgd->gsij", query_split, key_split, preferred_element_type=jnp.float32)
        * softmax_scale
    )
    scores = jnp.where(allowed[None, None], scores, NEG_FILL)
    row_top = jnp.max(scores, axis=-1, keepdims=True)
    row_total = jnp.sum(jnp.exp(scores - row_top), axis=-1, keepdims=True)
    probability = jnp.exp(scores - (row_top + jnp.log(row_total)))
    prob_low = probability.astype(jnp.bfloat16)
    attended = jnp.einsum(
        "gsij,jgd->igsd", prob_low, value_split, preferred_element_type=jnp.float32
    )
    delta = jnp.transpose(jnp.sum(grad_split.astype(jnp.float32) * attended, axis=-1), (1, 2, 0))
    dprob = jnp.einsum(
        "igsd,jgd->gsij", grad_split, value_split, preferred_element_type=jnp.float32
    )
    dscore_low = (probability * (dprob - delta[..., None])).astype(jnp.bfloat16)
    query_grad = (
        jnp.einsum("gsij,jgd->igsd", dscore_low, key_split, preferred_element_type=jnp.float32)
        * softmax_scale
    )
    query_grad = query_grad.reshape(rows_here, HEADS * HD).astype(jnp.bfloat16)
    key_term = (
        jnp.einsum("gsij,igsd->jgd", dscore_low, query_split, preferred_element_type=jnp.float32)
        * softmax_scale
    )
    value_term = jnp.einsum(
        "gsij,igsd->jgd", prob_low, grad_split, preferred_element_type=jnp.float32
    )
    summed_grads = lax.psum_scatter(
        jnp.concatenate(
            [
                key_term.reshape(lax.axis_size("ctx") * rows_here, key_width),
                value_term.reshape(lax.axis_size("ctx") * rows_here, key_width),
            ],
            axis=1,
        ),
        "ctx",
        scatter_dimension=0,
        tiled=True,
    )
    key_grad = summed_grads[:, :key_width].astype(jnp.bfloat16)
    value_grad = summed_grads[:, key_width:].astype(jnp.bfloat16)
    inputs_here = layer_inputs[0]
    weight_grad = lax.psum_scatter(
        jnp.einsum("te,tc->ec", inputs_here, value_grad, preferred_element_type=jnp.float32),
        ("dp", "ctx"),
        scatter_dimension=0,
        tiled=True,
    )
    weight_grad = weight_grad * (data_count * length) ** (-0.5)
    return (query_grad[None], key_grad[None], value_grad[None], weight_grad)


def place(query_heads, key_heads, value_heads, out_grad, layer_inputs, doc_lengths):
    arrays = (query_heads, key_heads, value_heads, out_grad, layer_inputs, doc_lengths)
    rows, model = layer_inputs.shape[1:]
    count = lax.axis_size("dp") * lax.axis_size("ctx")
    whole_tiles = rows % HD == 0 and model % (count * HD) == 0
    if lax.axis_size("ctx") == 2 and count == PLANE * KVH and whole_tiles:
        return fused(*arrays)
    return shards(*arrays)


def solution(mesh):
    placed = (
        P("dp", "ctx", None),
        P("dp", "ctx", None),
        P("dp", "ctx", None),
        P("dp", "ctx", None),
        P("dp", "ctx", None),
        P("dp", None),
    )
    return jax.shard_map(
        place,
        mesh=mesh,
        in_specs=placed,
        out_specs=(
            P("dp", "ctx", None),
            P("dp", "ctx", None),
            P("dp", "ctx", None),
            P(("dp", "ctx"), None),
        ),
        check_vma=False,
    )
```

```python
import functools
import math

import jax
import jax.numpy as jnp
from jax import lax
from jax.experimental import pallas as pl
from jax.experimental.pallas import tpu as pltpu
from jax.sharding import PartitionSpec as P

HD = 128
HEADS = 32
KVH = 4
GROUP = HEADS // KVH
PAIR = 2
PLANE = 8
LOG2E = math.log2(math.e)
F32 = jnp.float32
BF16 = jnp.bfloat16
MESH = pl.DeviceIdType.MESH


NEG_FILL = -1e30


def nt(a, b):
    return lax.dot_general(a, b, (((1,), (1,)), ((), ())), preferred_element_type=F32)


def nn(a, b):
    return jnp.dot(a, b, preferred_element_type=F32)


def cols(index, width=HD):
    return pl.ds(pl.multiple_of(index * width, width), width)


def target_orders(depth):
    table = []
    for z in range(depth):
        others = [t for t in range(depth) if t != z]
        others.sort(key=lambda t: (-abs(t - z), t))
        table.append(others + [z])
    return table


def documents_of(lengths, shape, axis, first):
    positions = lax.broadcasted_iota(jnp.int32, shape, axis) + first
    found = jnp.zeros(shape, jnp.int32)
    ending = jnp.int32(0)
    for number in range(lengths.shape[1]):
        ending = ending + lengths[0, number]
        found = found + (positions >= ending).astype(jnp.int32)
    return positions, found


def kernel(
    depth, out_scale,
    q_hbm, k_hbm, v_hbm, go_hbm, x_ref, len_ref,
    dq_ref, dk_ref, dv_ref, w_ref,
    q_ref, k_ref, v_ref, go_ref, k_prev, v_prev, bias, term_k, term_v,
    x_pack, x_all, dvt_all, w_send, w_recv, w_own,
    in_sem, kv_send, kv_recv, term_send, term_recv,
    x_send, x_recv, x_local, dv_send, dv_recv, ws_send, ws_recv,
):
    rows = q_ref.shape[0]
    dp = lax.axis_index("dp")
    ctx = lax.axis_index("ctx")
    lanes = PLANE // 2
    z = dp // lanes
    lane = dp % lanes
    me = lane * 2 + ctx
    width = w_ref.shape[0]
    scale = HD ** -0.5

    table = target_orders(depth)

    def target_at(step):
        target = jnp.int32(0)
        for place in range(depth):
            for number in range(depth):
                here = ((z == place) & (step == number)).astype(jnp.int32)
                target = target + here * table[place][number]
        return target

    targets = [target_at(step) for step in range(depth)]

    def pack_copy(target, offset):
        own = x_all.at[target, pl.ds(pl.multiple_of(me * rows, rows), rows)]
        return pltpu.make_async_copy(
            x_ref.at[:, cols(target * PLANE + (me + offset) % PLANE, width)],
            x_pack.at[target, offset] if offset else own,
            x_local.at[target, offset],
        )

    inputs = [
        pltpu.make_async_copy(src, dst, in_sem.at[i])
        for i, (src, dst) in enumerate(
            [(k_hbm, k_ref), (v_hbm, v_ref), (q_hbm, q_ref), (go_hbm, go_ref)]
        )
    ]
    for target in targets:
        for offset in [*range(2, PLANE, 2), *range(1, PLANE, 2), 0]:
            pack_copy(target, offset).start()
    for copy in inputs:
        copy.start()

    def peer(offset):
        other = (me + offset) % PLANE
        return other, (z * lanes + other // 2, other % 2)

    def level(target):
        return (target * lanes + lane, ctx)

    partner = (dp, 1 - ctx)

    barrier = pltpu.get_barrier_semaphore()
    for offset in range(1, PLANE):
        pl.semaphore_signal(barrier, inc=1, device_id=peer(offset)[1], device_id_type=MESH)
    for step in range(1, depth):
        pl.semaphore_signal(barrier, inc=1, device_id=level((z + step) % depth), device_id_type=MESH)
    pl.semaphore_wait(barrier, PLANE - 1 + depth - 1)

    def remote(src, dst, send, recv, device):
        return pltpu.make_async_remote_copy(
            src_ref=src, dst_ref=dst, send_sem=send, recv_sem=recv,
            device_id=device, device_id_type=MESH,
        )

    def kv_copy(g, part):
        src, dst = ((k_hbm, k_prev), (v_hbm, v_prev))[part]
        here = cols(g)
        return remote(src.at[:, here], dst.at[:, here], kv_send.at[part, g], kv_recv.at[part, g], partner)

    def term_copy(g, part):
        buffer = (term_v, term_k)[part].at[g]
        return remote(buffer, buffer, term_send.at[part, g], term_recv.at[part, g], partner)

    def x_copy(target, offset, sender, device):
        return remote(
            x_pack.at[target, offset],
            x_all.at[target, pl.ds(pl.multiple_of(sender * rows, rows), rows)],
            x_send.at[target, offset - 1], x_recv.at[target, offset - 1], device,
        )

    def flip(bits):
        row, core = (lane // 2 + bits // 4) % 2, (lane % 2 + bits // 2 % 2) % 2
        other = row * 4 + core * 2 + (ctx + bits % 2) % 2
        return other, (z * lanes + other // 2, other % 2)

    def dv_copy(g, bits, block, device):
        place = dvt_all.at[g, block]
        return remote(place, place, dv_send.at[g, bits - 1], dv_recv.at[g, bits - 1], device)

    def dv_direct(g):
        return [dv_copy(g, bits, me, flip(bits)[1]) for bits in (1, 4, 5, 2)]

    def dv_forward(g):
        return [dv_copy(g, bits + 2, flip(bits)[0], flip(2)[1]) for bits in (1, 4, 5)]

    def dv_arrived(g, kinds):
        for bits in kinds:
            other, device = flip(bits)
            dv_copy(g, bits, other, device).wait_recv()

    def forward(g):
        dv_arrived(g, (1, 4, 5))
        for copy in dv_forward(g):
            copy.start()

    def w_copy(g, source, target):
        here = cols(g)
        return remote(
            w_send.at[target, here], w_recv.at[source, here],
            ws_send.at[target, g], ws_recv.at[source, g], level(target),
        )

    @pl.when(ctx == 0)
    def _():
        for g in range(KVH):
            for part in range(2):
                kv_copy(g, part).start()

    def x_start(step, offset):
        x_copy(target_at(step), offset, me, peer(offset)[1]).start()

    def x_packed(step):
        for offset in range(1, PLANE):
            pack_copy(targets[step], offset).wait()

    x_packed(0)
    for offset in range(2, PLANE, 2):
        x_start(0, offset)

    @pl.when(ctx == 0)
    def _():
        for g in range(KVH):
            for part in range(2):
                kv_copy(g, part).wait_send()

    for offset in range(1, PLANE, 2):
        x_start(0, offset)
    for step in range(1, depth):
        x_packed(step)

    for copy in inputs:
        copy.wait()

    shape = (2 * rows, rows)
    first = ctx * rows
    query_pos, query_docs = documents_of(len_ref, shape, 1, first)
    key_pos, key_docs = documents_of(len_ref, shape, 0, first - rows)
    allowed = (query_docs == key_docs) & (key_pos <= query_pos)
    bias[...] = jnp.where(allowed, 0.0, NEG_FILL)

    def attend(g, blocks):
        length = blocks * rows
        here = cols(g)
        key_part, value_part = k_ref[:, here], v_ref[:, here]
        if blocks == 2:
            key_part = jnp.concatenate([k_prev[:, here], key_part], axis=0)
            value_part = jnp.concatenate([v_prev[:, here], value_part], axis=0)
        key_turned = key_part.astype(F32).T.astype(BF16)
        key_sum = jnp.zeros((length, HD), F32)
        value_sum = jnp.zeros((length, HD), F32)
        mask = jnp.concatenate([bias[2 * rows - length:]] * PAIR, axis=1)
        for pair in range(GROUP // PAIR):
            heads = [cols(g * GROUP + pair * PAIR + i) for i in range(PAIR)]
            query = jnp.concatenate([q_ref[:, h] for h in heads], axis=0)
            grad = jnp.concatenate([go_ref[:, h] for h in heads], axis=0)
            scores = nt(key_part, query) * (scale * LOG2E) + mask
            top = jnp.max(scores, axis=0, keepdims=True)
            weight = jnp.exp2(scores - top)
            prob = weight * (1.0 / jnp.sum(weight, axis=0, keepdims=True))
            prob_low = prob.astype(BF16)
            dprob = nt(value_part, grad)
            delta = jnp.sum(prob_low.astype(F32) * dprob, axis=0, keepdims=True)
            dscore = (prob * (dprob - delta)).astype(BF16)
            value_sum = value_sum + nn(prob_low, grad)
            key_sum = key_sum + nn(dscore, query)
            turned = nn(key_turned, dscore) * scale
            for i, h in enumerate(heads):
                dq_ref[:, h] = turned[:, i * rows:(i + 1) * rows].T.astype(BF16)
        return key_sum * scale, value_sum

    def finish(g, key_sum, value_sum):
        here = cols(g)
        dk_ref[:, here] = key_sum.astype(BF16)
        dv_ref[:, here] = value_sum.astype(BF16)
        dvt_all[g, me] = value_sum.T.astype(BF16)

    def gathered(g):
        return jnp.concatenate([dvt_all[g, sender] for sender in range(PLANE)], axis=1)

    def first_block(g):
        dv_arrived(g, (2, 3, 6, 7))
        target = targets[0]
        w_send[target, cols(g)] = nn(gathered(g), x_all[target]).astype(BF16)
        w_copy(g, z, target).start()

    def x_wait(target):
        for offset in range(1, PLANE):
            sender = (me + PLANE - offset) % PLANE
            x_copy(target, offset, sender, peer(offset)[1]).wait_recv()
        pack_copy(target, 0).wait()

    def group(g, carry):
        x_start(1, 2 * g + 1)

        @pl.when(2 * g + 2 < PLANE)
        def _():
            x_start(1, 2 * g + 2)

        @pl.when(ctx == 0)
        def _():
            key_sum, value_sum = attend(g, 1)
            for part in range(2):
                term_copy(g, part).wait_recv()
            finish(g, key_sum + term_k[g].astype(F32), value_sum + term_v[g].astype(F32))

        @pl.when(ctx == 1)
        def _():
            for part in range(2):
                kv_copy(g, part).wait_recv()
            key_sum, value_sum = attend(g, 2)
            term_v[g] = value_sum[:rows].astype(BF16)
            term_k[g] = key_sum[:rows].astype(BF16)
            for part in range(2):
                term_copy(g, part).start()
            finish(g, key_sum[rows:], value_sum[rows:])

        for copy in dv_direct(g):
            copy.start()

        @pl.when(g > 0)
        def _():
            forward(g - 1)

        @pl.when(g == 2)
        def _():
            x_wait(targets[0])

        @pl.when(g > 1)
        def _():
            first_block(g - 2)

        return carry

    lax.fori_loop(0, KVH, group, 0)
    forward(KVH - 1)
    for step in range(2, depth):
        for offset in range(1, PLANE):
            x_start(step, offset)
    first_block(KVH - 2)
    first_block(KVH - 1)

    def later(step, carry):
        target = target_at(step)
        x_wait(target)
        spread = jnp.concatenate([gathered(g) for g in range(KVH)], axis=0)
        w_send[target] = nn(spread, x_all[target]).astype(BF16)
        for g in range(KVH):
            w_copy(g, z, target).start()
        return carry

    lax.fori_loop(1, depth - 1, later, 0)
    x_wait(z)
    w_own[...] = nn(jnp.concatenate([gathered(g) for g in range(KVH)], axis=0), x_all[z])
    for step in range(1, depth):
        source = (z + step) % depth
        for g in range(KVH):
            w_copy(g, source, z).wait_recv()
        w_own[...] += w_recv[source].astype(F32)
    w_ref[...] = (w_own[...] * out_scale).T

    for target in targets:
        for offset in range(1, PLANE):
            x_copy(target, offset, me, peer(offset)[1]).wait_send()
    for step in range(1, depth):
        for g in range(KVH):
            w_copy(g, z, (z + step) % depth).wait_send()
    for g in range(KVH):
        for copy in dv_direct(g) + dv_forward(g):
            copy.wait_send()

    @pl.when(ctx == 1)
    def _():
        for g in range(KVH):
            for part in range(2):
                term_copy(g, part).wait_send()


def fused(query_heads, key_heads, value_heads, out_grad, layer_inputs, doc_lengths):
    rows, model = layer_inputs.shape[1:]
    key_width = key_heads.shape[2]
    count = lax.axis_size("dp") * lax.axis_size("ctx")
    depth = count // PLANE
    width = model // count
    out_scale = (lax.axis_size("dp") * lax.axis_size("ctx") * rows) ** (-0.5)
    vmem = pl.BlockSpec(memory_space=pltpu.VMEM)
    dma = pltpu.SemaphoreType.DMA
    query_grad, key_grad, value_grad, weight_grad = pl.pallas_call(
        functools.partial(kernel, depth, out_scale),
        out_shape=(
            jax.ShapeDtypeStruct(query_heads.shape[1:], BF16),
            jax.ShapeDtypeStruct((rows, key_width), BF16),
            jax.ShapeDtypeStruct((rows, key_width), BF16),
            jax.ShapeDtypeStruct((width, key_width), F32),
        ),
        in_specs=[pl.BlockSpec(memory_space=pltpu.HBM)] * 5 + [pl.BlockSpec(memory_space=pltpu.SMEM)],
        out_specs=(vmem,) * 4,
        scratch_shapes=[
            pltpu.VMEM(query_heads.shape[1:], BF16),
            pltpu.VMEM((rows, key_width), BF16),
            pltpu.VMEM((rows, key_width), BF16),
            pltpu.VMEM(query_heads.shape[1:], BF16),
            pltpu.VMEM((rows, key_width), BF16),
            pltpu.VMEM((rows, key_width), BF16),
            pltpu.VMEM((2 * rows, rows), F32),
            pltpu.VMEM((KVH, rows, HD), BF16),
            pltpu.VMEM((KVH, rows, HD), BF16),
            pltpu.VMEM((depth, PLANE, rows, width), BF16),
            pltpu.VMEM((depth, PLANE * rows, width), BF16),
            pltpu.VMEM((KVH, PLANE, HD, rows), BF16),
            pltpu.VMEM((depth, key_width, width), BF16),
            pltpu.VMEM((depth, key_width, width), BF16),
            pltpu.VMEM((key_width, width), F32),
            dma((4,)), dma((2, KVH)), dma((2, KVH)), dma((2, KVH)), dma((2, KVH)),
            dma((depth, PLANE - 1)), dma((depth, PLANE - 1)), dma((depth, PLANE)),
            dma((KVH, PLANE - 1)), dma((KVH, PLANE - 1)),
            dma((depth, KVH)), dma((depth, KVH)),
        ],
        compiler_params=pltpu.CompilerParams(
            collective_id=0, has_side_effects=True, vmem_limit_bytes=64 * 1024 * 1024
        ),
    )(query_heads[0], key_heads[0], value_heads[0], out_grad[0], layer_inputs[0], doc_lengths)
    return (query_grad[None], key_grad[None], value_grad[None], weight_grad)


def document_ids(lengths_row, length):
    endings = jnp.cumsum(lengths_row)
    positions = jnp.arange(length, dtype=jnp.int32)
    return jnp.sum((positions[:, None] >= endings[None, :]).astype(jnp.int32), axis=1)


def shards(query_heads, key_heads, value_heads, out_grad, layer_inputs, doc_lengths):
    queries_here = query_heads[0]
    rows_here = queries_here.shape[0]
    shard_count = lax.axis_size("ctx")
    data_count = lax.axis_size("dp")
    length = rows_here * shard_count
    group_size = HEADS // KVH
    softmax_scale = HD ** (-0.5)
    key_width = key_heads.shape[2]
    key_all, value_all = (
        lax.all_gather(key_heads[0], "ctx", axis=0, tiled=True),
        lax.all_gather(value_heads[0], "ctx", axis=0, tiled=True),
    )
    documents = document_ids(doc_lengths[0], length)
    first_row = lax.axis_index("ctx") * rows_here
    positions = jnp.arange(length, dtype=jnp.int32)
    query_pos = first_row + jnp.arange(rows_here, dtype=jnp.int32)
    query_docs = lax.dynamic_slice_in_dim(documents, first_row, rows_here)
    allowed = (query_docs[:, None] == documents[None, :]) & (
        positions[None, :] <= query_pos[:, None]
    )
    query_split = queries_here.reshape(rows_here, KVH, group_size, HD)
    key_split = key_all.reshape(length, KVH, HD)
    value_split = value_all.reshape(length, KVH, HD)
    grad_split = out_grad[0].reshape(rows_here, KVH, group_size, HD)
    scores = (
        jnp.einsum("igsd,jgd->gsij", query_split, key_split, preferred_element_type=jnp.float32)
        * softmax_scale
    )
    scores = jnp.where(allowed[None, None], scores, NEG_FILL)
    row_top = jnp.max(scores, axis=-1, keepdims=True)
    row_total = jnp.sum(jnp.exp(scores - row_top), axis=-1, keepdims=True)
    probability = jnp.exp(scores - (row_top + jnp.log(row_total)))
    prob_low = probability.astype(jnp.bfloat16)
    attended = jnp.einsum(
        "gsij,jgd->igsd", prob_low, value_split, preferred_element_type=jnp.float32
    )
    delta = jnp.transpose(jnp.sum(grad_split.astype(jnp.float32) * attended, axis=-1), (1, 2, 0))
    dprob = jnp.einsum(
        "igsd,jgd->gsij", grad_split, value_split, preferred_element_type=jnp.float32
    )
    dscore_low = (probability * (dprob - delta[..., None])).astype(jnp.bfloat16)
    query_grad = (
        jnp.einsum("gsij,jgd->igsd", dscore_low, key_split, preferred_element_type=jnp.float32)
        * softmax_scale
    )
    query_grad = query_grad.reshape(rows_here, HEADS * HD).astype(jnp.bfloat16)
    key_term = (
        jnp.einsum("gsij,igsd->jgd", dscore_low, query_split, preferred_element_type=jnp.float32)
        * softmax_scale
    )
    value_term = jnp.einsum(
        "gsij,igsd->jgd", prob_low, grad_split, preferred_element_type=jnp.float32
    )
    summed_grads = lax.psum_scatter(
        jnp.concatenate(
            [
                key_term.reshape(lax.axis_size("ctx") * rows_here, key_width),
                value_term.reshape(lax.axis_size("ctx") * rows_here, key_width),
            ],
            axis=1,
        ),
        "ctx",
        scatter_dimension=0,
        tiled=True,
    )
    key_grad = summed_grads[:, :key_width].astype(jnp.bfloat16)
    value_grad = summed_grads[:, key_width:].astype(jnp.bfloat16)
    inputs_here = layer_inputs[0]
    weight_grad = lax.psum_scatter(
        jnp.einsum("te,tc->ec", inputs_here, value_grad, preferred_element_type=jnp.float32),
        ("dp", "ctx"),
        scatter_dimension=0,
        tiled=True,
    )
    weight_grad = weight_grad * (data_count * length) ** (-0.5)
    return (query_grad[None], key_grad[None], value_grad[None], weight_grad)


def place(query_heads, key_heads, value_heads, out_grad, layer_inputs, doc_lengths):
    arrays = (query_heads, key_heads, value_heads, out_grad, layer_inputs, doc_lengths)
    rows, model = layer_inputs.shape[1:]
    count = lax.axis_size("dp") * lax.axis_size("ctx")
    whole_tiles = rows % HD == 0 and model % (count * HD) == 0
    if lax.axis_size("ctx") == 2 and count == PLANE * KVH and whole_tiles:
        return fused(*arrays)
    return shards(*arrays)


def solution(mesh):
    placed = (
        P("dp", "ctx", None),
        P("dp", "ctx", None),
        P("dp", "ctx", None),
        P("dp", "ctx", None),
        P("dp", "ctx", None),
        P("dp", None),
    )
    return jax.shard_map(
        place,
        mesh=mesh,
        in_specs=placed,
        out_specs=(
            P("dp", "ctx", None),
            P("dp", "ctx", None),
            P("dp", "ctx", None),
            P(("dp", "ctx"), None),
        ),
        check_vma=False,
    )
```

```python
import functools
import math

import jax
import jax.numpy as jnp
from jax import lax
from jax.experimental import pallas as pl
from jax.experimental.pallas import tpu as pltpu
from jax.sharding import PartitionSpec as P

HD = 128
HEADS = 32
KVH = 4
GROUP = HEADS // KVH
PAIR = 2
PLANE = 8
PACE = 3
LOG2E = math.log2(math.e)
F32 = jnp.float32
BF16 = jnp.bfloat16
MESH = pl.DeviceIdType.MESH


NEG_FILL = -1e30


def nt(a, b):
    return lax.dot_general(a, b, (((1,), (1,)), ((), ())), preferred_element_type=F32)


def nn(a, b):
    return jnp.dot(a, b, preferred_element_type=F32)


def cols(index, width=HD):
    return pl.ds(pl.multiple_of(index * width, width), width)


def target_orders(depth):
    table = []
    for z in range(depth):
        others = [t for t in range(depth) if t != z]
        others.sort(key=lambda t: (-abs(t - z), t))
        table.append(others + [z])
    return table


def documents_of(lengths, shape, axis, first):
    positions = lax.broadcasted_iota(jnp.int32, shape, axis) + first
    found = jnp.zeros(shape, jnp.int32)
    ending = jnp.int32(0)
    for number in range(lengths.shape[1]):
        ending = ending + lengths[0, number]
        found = found + (positions >= ending).astype(jnp.int32)
    return positions, found


def kernel(
    depth, out_scale,
    q_hbm, k_hbm, v_hbm, go_hbm, x_ref, len_ref,
    dq_ref, dk_ref, dv_ref, w_ref,
    q_ref, k_ref, v_ref, go_ref, k_prev, v_prev, bias, term_k, term_v,
    x_pack, x_all, dvt_all, w_send, w_recv, w_own,
    in_sem, kv_send, kv_recv, term_send, term_recv,
    x_send, x_recv, x_local, dv_send, dv_recv, ws_send, ws_recv,
):
    rows = q_ref.shape[0]
    dp = lax.axis_index("dp")
    ctx = lax.axis_index("ctx")
    lanes = PLANE // 2
    z = dp // lanes
    lane = dp % lanes
    me = lane * 2 + ctx
    width = w_ref.shape[0]
    scale = HD ** -0.5

    table = target_orders(depth)

    def target_at(step):
        target = jnp.int32(0)
        for place in range(depth):
            for number in range(depth):
                here = ((z == place) & (step == number)).astype(jnp.int32)
                target = target + here * table[place][number]
        return target

    targets = [target_at(step) for step in range(depth)]

    def pack_copy(target, offset):
        own = x_all.at[target, pl.ds(pl.multiple_of(me * rows, rows), rows)]
        return pltpu.make_async_copy(
            x_ref.at[:, cols(target * PLANE + (me + offset) % PLANE, width)],
            x_pack.at[target, offset] if offset else own,
            x_local.at[target, offset],
        )

    inputs = [
        pltpu.make_async_copy(src, dst, in_sem.at[i])
        for i, (src, dst) in enumerate(
            [(k_hbm, k_ref), (v_hbm, v_ref), (q_hbm, q_ref), (go_hbm, go_ref)]
        )
    ]
    for target in targets:
        for offset in [*range(2, PLANE, 2), *range(1, PLANE, 2), 0]:
            pack_copy(target, offset).start()
    for copy in inputs:
        copy.start()

    def peer(offset):
        other = (me + offset) % PLANE
        return other, (z * lanes + other // 2, other % 2)

    def level(target):
        return (target * lanes + lane, ctx)

    partner = (dp, 1 - ctx)

    barrier = pltpu.get_barrier_semaphore()
    for offset in range(1, PLANE):
        pl.semaphore_signal(barrier, inc=1, device_id=peer(offset)[1], device_id_type=MESH)
    for step in range(1, depth):
        pl.semaphore_signal(barrier, inc=1, device_id=level((z + step) % depth), device_id_type=MESH)
    pl.semaphore_wait(barrier, PLANE - 1 + depth - 1)

    def remote(src, dst, send, recv, device):
        return pltpu.make_async_remote_copy(
            src_ref=src, dst_ref=dst, send_sem=send, recv_sem=recv,
            device_id=device, device_id_type=MESH,
        )

    def kv_copy(g, part):
        src, dst = ((k_hbm, k_prev), (v_hbm, v_prev))[part]
        here = cols(g)
        return remote(src.at[:, here], dst.at[:, here], kv_send.at[part, g], kv_recv.at[part, g], partner)

    def term_copy(g, part):
        buffer = (term_v, term_k)[part].at[g]
        return remote(buffer, buffer, term_send.at[part, g], term_recv.at[part, g], partner)

    def x_copy(target, offset, sender, device):
        return remote(
            x_pack.at[target, offset],
            x_all.at[target, pl.ds(pl.multiple_of(sender * rows, rows), rows)],
            x_send.at[target, offset - 1], x_recv.at[target, offset - 1], device,
        )

    def flip(bits):
        row, core = (lane // 2 + bits // 4) % 2, (lane % 2 + bits // 2 % 2) % 2
        other = row * 4 + core * 2 + (ctx + bits % 2) % 2
        return other, (z * lanes + other // 2, other % 2)

    def dv_copy(g, bits, block, device):
        place = dvt_all.at[g, block]
        return remote(place, place, dv_send.at[g, bits - 1], dv_recv.at[g, bits - 1], device)

    def dv_direct(g):
        return [dv_copy(g, bits, me, flip(bits)[1]) for bits in (1, 4, 5, 2)]

    def dv_forward(g):
        return [dv_copy(g, bits + 2, flip(bits)[0], flip(2)[1]) for bits in (1, 4, 5)]

    def dv_arrived(g, kinds):
        for bits in kinds:
            other, device = flip(bits)
            dv_copy(g, bits, other, device).wait_recv()

    def forward(g):
        dv_arrived(g, (1, 4, 5))
        for copy in dv_forward(g):
            copy.start()

    def w_copy(g, source, target):
        here = cols(g)
        return remote(
            w_send.at[target, here], w_recv.at[source, here],
            ws_send.at[target, g], ws_recv.at[source, g], level(target),
        )

    @pl.when(ctx == 0)
    def _():
        for g in range(KVH):
            for part in range(2):
                kv_copy(g, part).start()

    def x_start(step, offset):
        x_copy(target_at(step), offset, me, peer(offset)[1]).start()

    def x_packed(step):
        for offset in range(1, PLANE):
            pack_copy(targets[step], offset).wait()

    x_packed(0)
    for offset in range(2, PLANE, 2):
        x_start(0, offset)

    @pl.when(ctx == 0)
    def _():
        for g in range(KVH):
            for part in range(2):
                kv_copy(g, part).wait_send()

    for offset in range(1, PLANE, 2):
        x_start(0, offset)
    for step in range(1, depth):
        x_packed(step)

    for copy in inputs:
        copy.wait()

    shape = (2 * rows, rows)
    first = ctx * rows
    query_pos, query_docs = documents_of(len_ref, shape, 1, first)
    key_pos, key_docs = documents_of(len_ref, shape, 0, first - rows)
    allowed = (query_docs == key_docs) & (key_pos <= query_pos)
    bias[...] = jnp.where(allowed, 0.0, NEG_FILL)

    def attend(g, blocks):
        length = blocks * rows
        here = cols(g)
        key_part, value_part = k_ref[:, here], v_ref[:, here]
        if blocks == 2:
            key_part = jnp.concatenate([k_prev[:, here], key_part], axis=0)
            value_part = jnp.concatenate([v_prev[:, here], value_part], axis=0)
        key_turned = key_part.astype(F32).T.astype(BF16)
        key_sum = jnp.zeros((length, HD), F32)
        value_sum = jnp.zeros((length, HD), F32)
        mask = jnp.concatenate([bias[2 * rows - length:]] * PAIR, axis=1)
        for pair in range(GROUP // PAIR):
            heads = [cols(g * GROUP + pair * PAIR + i) for i in range(PAIR)]
            query = jnp.concatenate([q_ref[:, h] for h in heads], axis=0)
            grad = jnp.concatenate([go_ref[:, h] for h in heads], axis=0)
            scores = nt(key_part, query) * (scale * LOG2E) + mask
            top = jnp.max(scores, axis=0, keepdims=True)
            weight = jnp.exp2(scores - top)
            prob = weight * (1.0 / jnp.sum(weight, axis=0, keepdims=True))
            prob_low = prob.astype(BF16)
            dprob = nt(value_part, grad)
            delta = jnp.sum(prob_low.astype(F32) * dprob, axis=0, keepdims=True)
            dscore = (prob * (dprob - delta)).astype(BF16)
            value_sum = value_sum + nn(prob_low, grad)
            key_sum = key_sum + nn(dscore, query)
            turned = nn(key_turned, dscore) * scale
            for i, h in enumerate(heads):
                dq_ref[:, h] = turned[:, i * rows:(i + 1) * rows].T.astype(BF16)
        return key_sum * scale, value_sum

    def finish(g, key_sum, value_sum):
        here = cols(g)
        dk_ref[:, here] = key_sum.astype(BF16)
        dv_ref[:, here] = value_sum.astype(BF16)
        dvt_all[g, me] = value_sum.T.astype(BF16)

    def gathered(g):
        return jnp.concatenate([dvt_all[g, sender] for sender in range(PLANE)], axis=1)

    def first_block(g):
        dv_arrived(g, (2, 3, 6, 7))
        target = targets[0]
        w_send[target, cols(g)] = nn(gathered(g), x_all[target]).astype(BF16)
        w_copy(g, z, target).start()

    def x_wait(target):
        for offset in range(1, PLANE):
            sender = (me + PLANE - offset) % PLANE
            x_copy(target, offset, sender, peer(offset)[1]).wait_recv()
        pack_copy(target, 0).wait()

    def group(g, carry):
        for part in range(PACE):
            number = g * PACE + part
            x_start(1 + number // (PLANE - 1), number % (PLANE - 1) + 1)

        @pl.when(ctx == 0)
        def _():
            key_sum, value_sum = attend(g, 1)
            for part in range(2):
                term_copy(g, part).wait_recv()
            finish(g, key_sum + term_k[g].astype(F32), value_sum + term_v[g].astype(F32))

        @pl.when(ctx == 1)
        def _():
            for part in range(2):
                kv_copy(g, part).wait_recv()
            key_sum, value_sum = attend(g, 2)
            term_v[g] = value_sum[:rows].astype(BF16)
            term_k[g] = key_sum[:rows].astype(BF16)
            for part in range(2):
                term_copy(g, part).start()
            finish(g, key_sum[rows:], value_sum[rows:])

        for copy in dv_direct(g):
            copy.start()

        @pl.when(g > 0)
        def _():
            forward(g - 1)

        @pl.when(g == 2)
        def _():
            x_wait(targets[0])

        @pl.when(g > 1)
        def _():
            first_block(g - 2)

        return carry

    lax.fori_loop(0, KVH, group, 0)
    forward(KVH - 1)
    for number in range(KVH * PACE, (depth - 1) * (PLANE - 1)):
        x_start(1 + number // (PLANE - 1), number % (PLANE - 1) + 1)
    first_block(KVH - 2)
    first_block(KVH - 1)

    def later(step, carry):
        target = target_at(step)
        x_wait(target)
        spread = jnp.concatenate([gathered(g) for g in range(KVH)], axis=0)
        w_send[target] = nn(spread, x_all[target]).astype(BF16)
        for g in range(KVH):
            w_copy(g, z, target).start()
        return carry

    lax.fori_loop(1, depth - 1, later, 0)
    x_wait(z)
    w_own[...] = nn(jnp.concatenate([gathered(g) for g in range(KVH)], axis=0), x_all[z])
    for step in range(1, depth):
        source = (z + step) % depth
        for g in range(KVH):
            w_copy(g, source, z).wait_recv()
        w_own[...] += w_recv[source].astype(F32)
    w_ref[...] = (w_own[...] * out_scale).T

    for target in targets:
        for offset in range(1, PLANE):
            x_copy(target, offset, me, peer(offset)[1]).wait_send()
    for step in range(1, depth):
        for g in range(KVH):
            w_copy(g, z, (z + step) % depth).wait_send()
    for g in range(KVH):
        for copy in dv_direct(g) + dv_forward(g):
            copy.wait_send()

    @pl.when(ctx == 1)
    def _():
        for g in range(KVH):
            for part in range(2):
                term_copy(g, part).wait_send()


def fused(query_heads, key_heads, value_heads, out_grad, layer_inputs, doc_lengths):
    rows, model = layer_inputs.shape[1:]
    key_width = key_heads.shape[2]
    count = lax.axis_size("dp") * lax.axis_size("ctx")
    depth = count // PLANE
    width = model // count
    out_scale = (lax.axis_size("dp") * lax.axis_size("ctx") * rows) ** (-0.5)
    vmem = pl.BlockSpec(memory_space=pltpu.VMEM)
    dma = pltpu.SemaphoreType.DMA
    query_grad, key_grad, value_grad, weight_grad = pl.pallas_call(
        functools.partial(kernel, depth, out_scale),
        out_shape=(
            jax.ShapeDtypeStruct(query_heads.shape[1:], BF16),
            jax.ShapeDtypeStruct((rows, key_width), BF16),
            jax.ShapeDtypeStruct((rows, key_width), BF16),
            jax.ShapeDtypeStruct((width, key_width), F32),
        ),
        in_specs=[pl.BlockSpec(memory_space=pltpu.HBM)] * 5 + [pl.BlockSpec(memory_space=pltpu.SMEM)],
        out_specs=(vmem,) * 4,
        scratch_shapes=[
            pltpu.VMEM(query_heads.shape[1:], BF16),
            pltpu.VMEM((rows, key_width), BF16),
            pltpu.VMEM((rows, key_width), BF16),
            pltpu.VMEM(query_heads.shape[1:], BF16),
            pltpu.VMEM((rows, key_width), BF16),
            pltpu.VMEM((rows, key_width), BF16),
            pltpu.VMEM((2 * rows, rows), F32),
            pltpu.VMEM((KVH, rows, HD), BF16),
            pltpu.VMEM((KVH, rows, HD), BF16),
            pltpu.VMEM((depth, PLANE, rows, width), BF16),
            pltpu.VMEM((depth, PLANE * rows, width), BF16),
            pltpu.VMEM((KVH, PLANE, HD, rows), BF16),
            pltpu.VMEM((depth, key_width, width), BF16),
            pltpu.VMEM((depth, key_width, width), BF16),
            pltpu.VMEM((key_width, width), F32),
            dma((4,)), dma((2, KVH)), dma((2, KVH)), dma((2, KVH)), dma((2, KVH)),
            dma((depth, PLANE - 1)), dma((depth, PLANE - 1)), dma((depth, PLANE)),
            dma((KVH, PLANE - 1)), dma((KVH, PLANE - 1)),
            dma((depth, KVH)), dma((depth, KVH)),
        ],
        compiler_params=pltpu.CompilerParams(
            collective_id=0, has_side_effects=True, vmem_limit_bytes=64 * 1024 * 1024
        ),
    )(query_heads[0], key_heads[0], value_heads[0], out_grad[0], layer_inputs[0], doc_lengths)
    return (query_grad[None], key_grad[None], value_grad[None], weight_grad)


def document_ids(lengths_row, length):
    endings = jnp.cumsum(lengths_row)
    positions = jnp.arange(length, dtype=jnp.int32)
    return jnp.sum((positions[:, None] >= endings[None, :]).astype(jnp.int32), axis=1)


def shards(query_heads, key_heads, value_heads, out_grad, layer_inputs, doc_lengths):
    queries_here = query_heads[0]
    rows_here = queries_here.shape[0]
    shard_count = lax.axis_size("ctx")
    data_count = lax.axis_size("dp")
    length = rows_here * shard_count
    group_size = HEADS // KVH
    softmax_scale = HD ** (-0.5)
    key_width = key_heads.shape[2]
    key_all, value_all = (
        lax.all_gather(key_heads[0], "ctx", axis=0, tiled=True),
        lax.all_gather(value_heads[0], "ctx", axis=0, tiled=True),
    )
    documents = document_ids(doc_lengths[0], length)
    first_row = lax.axis_index("ctx") * rows_here
    positions = jnp.arange(length, dtype=jnp.int32)
    query_pos = first_row + jnp.arange(rows_here, dtype=jnp.int32)
    query_docs = lax.dynamic_slice_in_dim(documents, first_row, rows_here)
    allowed = (query_docs[:, None] == documents[None, :]) & (
        positions[None, :] <= query_pos[:, None]
    )
    query_split = queries_here.reshape(rows_here, KVH, group_size, HD)
    key_split = key_all.reshape(length, KVH, HD)
    value_split = value_all.reshape(length, KVH, HD)
    grad_split = out_grad[0].reshape(rows_here, KVH, group_size, HD)
    scores = (
        jnp.einsum("igsd,jgd->gsij", query_split, key_split, preferred_element_type=jnp.float32)
        * softmax_scale
    )
    scores = jnp.where(allowed[None, None], scores, NEG_FILL)
    row_top = jnp.max(scores, axis=-1, keepdims=True)
    row_total = jnp.sum(jnp.exp(scores - row_top), axis=-1, keepdims=True)
    probability = jnp.exp(scores - (row_top + jnp.log(row_total)))
    prob_low = probability.astype(jnp.bfloat16)
    attended = jnp.einsum(
        "gsij,jgd->igsd", prob_low, value_split, preferred_element_type=jnp.float32
    )
    delta = jnp.transpose(jnp.sum(grad_split.astype(jnp.float32) * attended, axis=-1), (1, 2, 0))
    dprob = jnp.einsum(
        "igsd,jgd->gsij", grad_split, value_split, preferred_element_type=jnp.float32
    )
    dscore_low = (probability * (dprob - delta[..., None])).astype(jnp.bfloat16)
    query_grad = (
        jnp.einsum("gsij,jgd->igsd", dscore_low, key_split, preferred_element_type=jnp.float32)
        * softmax_scale
    )
    query_grad = query_grad.reshape(rows_here, HEADS * HD).astype(jnp.bfloat16)
    key_term = (
        jnp.einsum("gsij,igsd->jgd", dscore_low, query_split, preferred_element_type=jnp.float32)
        * softmax_scale
    )
    value_term = jnp.einsum(
        "gsij,igsd->jgd", prob_low, grad_split, preferred_element_type=jnp.float32
    )
    summed_grads = lax.psum_scatter(
        jnp.concatenate(
            [
                key_term.reshape(lax.axis_size("ctx") * rows_here, key_width),
                value_term.reshape(lax.axis_size("ctx") * rows_here, key_width),
            ],
            axis=1,
        ),
        "ctx",
        scatter_dimension=0,
        tiled=True,
    )
    key_grad = summed_grads[:, :key_width].astype(jnp.bfloat16)
    value_grad = summed_grads[:, key_width:].astype(jnp.bfloat16)
    inputs_here = layer_inputs[0]
    weight_grad = lax.psum_scatter(
        jnp.einsum("te,tc->ec", inputs_here, value_grad, preferred_element_type=jnp.float32),
        ("dp", "ctx"),
        scatter_dimension=0,
        tiled=True,
    )
    weight_grad = weight_grad * (data_count * length) ** (-0.5)
    return (query_grad[None], key_grad[None], value_grad[None], weight_grad)


def place(query_heads, key_heads, value_heads, out_grad, layer_inputs, doc_lengths):
    arrays = (query_heads, key_heads, value_heads, out_grad, layer_inputs, doc_lengths)
    rows, model = layer_inputs.shape[1:]
    count = lax.axis_size("dp") * lax.axis_size("ctx")
    whole_tiles = rows % HD == 0 and model % (count * HD) == 0
    if lax.axis_size("ctx") == 2 and count == PLANE * KVH and whole_tiles:
        return fused(*arrays)
    return shards(*arrays)


def solution(mesh):
    placed = (
        P("dp", "ctx", None),
        P("dp", "ctx", None),
        P("dp", "ctx", None),
        P("dp", "ctx", None),
        P("dp", "ctx", None),
        P("dp", None),
    )
    return jax.shard_map(
        place,
        mesh=mesh,
        in_specs=placed,
        out_specs=(
            P("dp", "ctx", None),
            P("dp", "ctx", None),
            P("dp", "ctx", None),
            P(("dp", "ctx"), None),
        ),
        check_vma=False,
    )
```
